128 devices in a mesh: ep: 16 (over z, y), fsdp: 8 (over x, core).
Axes of the slice: x: 4, y: 4, z: 4, core: 2. Of those that a mesh axis runs over, the one named last changes fastest.
Arguments:
- tokens: bfloat16 [2048, 7168], P('ep'), may hold values from -6 to 6
- w_gate: bfloat16 [16, 7168, 2048], P('ep', None, 'fsdp'), may hold values from -0.0625 to 0.0625
- w_up: bfloat16 [16, 7168, 2048], P('ep', None, 'fsdp'), may hold values from -0.0625 to 0.0625
- tangent_down: bfloat16 [16, 2048, 7168], P('ep', 'fsdp'), may hold values from -0.1875 to 0.1875
- gates: float32 [2048, 2], P('ep'), may hold values from 0.1 to 1
- expert_ids: int32 [2048, 2], P('ep'), may hold values from 0 to 15, all different within a row; in each aligned block of 128 rows (0 to 127, 128 to 255, ...) at most 32 rows name the same one
Outputs:
- gn_product: float32 [16, 2048, 7168], P('ep', 'fsdp')
- tangent: bfloat16 [2048, 7168], P('ep', 'fsdp')
The draws below stay inside these ranges and needn't reach their ends.
Inputs may be any that keep to these rules, and one draw needn't show every extreme that they name: `expert_ids`: each row names 2 different experts. Within the rows of one index of ep (128 tokens) no expert is named by more than 32 routes, a bound that some block reaches.
All inputs are finite; a program needn't handle non-finite values.
Results may differ from the reference program's by a relative error of at most 0.022.
Values may be sent and summed in bfloat16 or wider, within the bound.
A program may use at most 128 MiB of HBM per device.

```python
import math
import jax
import jax.numpy as jnp
import numpy as np
from jax import lax

D = 7168
FF = 2048
TOK_DEV = 128
TOPK = 2
EXPERTS = 16
TOKENS = 2048
CAP = 32


def with_spikes(array, rng, source, target, parts, factor):
    owner, partner = [(jnp.arange(array.shape[position]) // (array.shape[position] // parts)).reshape([-1 if axis == position else 1 for axis in range(array.ndim)]) for position in (source, target)]
    chosen = jax.random.permutation(rng, parts)[partner]
    strong = (owner == chosen) | (owner == (partner + parts // 2) % parts)
    return jnp.where(strong, factor * array, array)


def level_of(own_key, dims, shards, smallest, high):
    def one(axis_at, blocks):
        draws = jax.random.uniform(jax.random.fold_in(jax.random.fold_in(own_key, 6), axis_at), (blocks,), jnp.float32, smallest / len(shards), high / len(shards))
        return jnp.repeat(jnp.exp(draws), dims[axis_at] // blocks).reshape((-1,) + (1,) * (len(dims) - axis_at - 1))

    loudness = one(*shards[0])
    for cut in shards[1:]:
        loudness = loudness * one(*cut)
    return loudness


def shared_out(key, own, number, rows, number_of, top, limit, slope):
    sequence = jax.random.permutation(key, number_of)
    packed, usual = shares(number_of, rows * top, limit, slope, True), shares(number_of, rows * top, limit, slope, False)
    places = jnp.arange(number_of)

    def named(sizes, turn):
        used = int((sizes > 0).sum())
        fixed = max(1, used // 4)
        passed = fixed + (places - fixed + turn * (used - fixed)) % max(1, number_of - fixed)
        return jnp.zeros((number_of,), jnp.int32).at[sequence[jnp.where(places < fixed, places, passed)]].set(jnp.asarray(sizes, jnp.int32))

    sizes = jnp.where(number % 4 == 0, named(packed, number // 4), named(usual, number - number // 4 - 1))
    mixed = jax.random.permutation(jax.random.fold_in(own, 3), number_of)
    donor, taker = mixed[0:number_of // 2 * 2:2], mixed[1:number_of // 2 * 2:2]
    slack = jnp.minimum(sizes[donor] - 1, limit - sizes[taker]) // 2
    slack = jnp.where((donor == sequence[0]) | (taker == sequence[0]) | (sizes[taker] == 0), 0, jnp.maximum(slack, 0))
    passed = jax.random.randint(jax.random.fold_in(own, 4), (number_of // 2,), 0, 1 << 20) % (slack + 1)
    sizes = sizes.at[donor].add(-passed).at[taker].add(passed)
    items = jnp.searchsorted(jnp.cumsum(sizes), jnp.arange(rows * top), side="right").astype(jnp.int32)
    grid = items.reshape(top, rows).T
    grid = grid[jax.random.permutation(jax.random.fold_in(own, 1), rows)]
    turn = jax.random.randint(jax.random.fold_in(own, 2), (rows, 1), 0, top)
    return jnp.take_along_axis(grid, (jnp.arange(top)[None, :] + turn) % top, axis=1)


def shares(number_of, total, limit, skew, full):
    weights = [(1 << 20) // math.isqrt(standing ** skew) + 1 for standing in range(1, number_of + 1)]
    largest = limit if full else min(limit, max(-(-total // number_of), total * weights[0] // sum(weights)))
    least = 1 if total - largest >= number_of - 1 else 0
    counts, surplus = [largest] + [least] * (number_of - 1), total - largest - least * (number_of - 1)
    while surplus > 0:
        candidates = [i for i in range(1, number_of) if counts[i] < largest] or [i for i in range(1, number_of) if counts[i] < limit]
        pool, left = sum([weights[i] for i in candidates]), surplus
        for i in candidates:
            extra = min(limit - counts[i], max(1, left * weights[i] // pool), surplus)
            counts[i] = counts[i] + extra
            surplus = surplus - extra
    return np.array(counts)


def scatter_about(own_key, dims, deviation, bound, shards=(), held_as=jnp.bfloat16):
    entries = jax.random.normal(own_key, dims, jnp.float32) * deviation
    if len(shards) > 0:
        entries = level_of(own_key, dims, shards, -0.22, 0.18) * entries
    return jnp.clip(entries, min=-bound, max=bound).astype(held_as)


def gaussian_with(own_key, extent, scale, limit, pieces, heavy, kind=jnp.bfloat16):
    values = scale * jax.random.normal(own_key, extent, jnp.float32)
    if pieces:
        values = values * level_of(own_key, extent, pieces, -0.22, 0.18)
    return jnp.clip(with_spikes(values, jax.random.fold_in(own_key, 3), *heavy), -limit, limit).astype(kind)


def setup_inputs(seed: int = 0) -> dict:
    keys = jax.random.split(jax.random.key(seed), 7)
    tokens = scatter_about(keys[0], (TOKENS, D), 1.0, 6.0, ((0, 16),))
    w_gate = scatter_about(keys[1], (EXPERTS, D, FF), D ** -0.5, 0.0625, ((0, 16), (2, 8)))
    w_up = scatter_about(keys[2], (EXPERTS, D, FF), D ** -0.5, 0.0625, ((0, 16), (2, 8)))
    tangent_down = gaussian_with(keys[3], (EXPERTS, FF, D), FF ** -0.5, 0.1875, ((0, 16), (1, 8)), (1, 2, 8, 2.0))
    gates = jnp.clip(jnp.exp(math.log(1.0) - 2.3025851 * jax.random.uniform(keys[4], (TOKENS, TOPK), jnp.float32) ** level_of(keys[4], (TOKENS, TOPK), ((0, 16),), -0.2, 0.2)), 0.1, 1.0)
    expert_ids_keys = jax.random.split(jax.random.fold_in(keys[5], 1), TOKENS // TOK_DEV)
    expert_ids_turns = jax.random.permutation(jax.random.fold_in(keys[5], 3), TOKENS // TOK_DEV)
    expert_ids = jax.vmap(lambda own, number: shared_out(jax.random.fold_in(keys[5], 2), own, number, TOK_DEV, EXPERTS, TOPK, CAP, 2))(expert_ids_keys, expert_ids_turns).reshape((TOKENS, TOPK))
    return dict(tokens=tokens, w_gate=w_gate, w_up=w_up, tangent_down=tangent_down, gates=gates, expert_ids=expert_ids)


def reference(tokens, w_gate, w_up, tangent_down, gates, expert_ids):
    def expert_hidden(index):
        first = jnp.dot(tokens, w_gate[index], preferred_element_type=jnp.float32)
        second = jnp.dot(tokens, w_up[index], preferred_element_type=jnp.float32)
        return (jax.nn.silu(first) * second).astype(jnp.bfloat16)

    def weight_of(index):
        return jnp.sum(jnp.where(expert_ids == index, gates, jnp.zeros_like(gates)), axis=1)

    order = jnp.arange(EXPERTS).astype(jnp.int32)
    hidden_all = lax.map(expert_hidden, order)

    def forward(total, index):
        product = jnp.dot(hidden_all[index], tangent_down[index], preferred_element_type=jnp.float32)
        return total + weight_of(index)[:, None] * product, None

    start = jnp.zeros((TOKENS, D), jnp.float32)
    tangent_sum, _ = lax.scan(forward, start, order)
    tangent = tangent_sum.astype(jnp.bfloat16)

    def backward(index):
        weighted = (weight_of(index)[:, None] * tangent.astype(jnp.float32)).astype(jnp.bfloat16)
        return lax.dot_general(hidden_all[index], weighted, (((0,), (0,)), ((), ())), preferred_element_type=jnp.float32)

    gn_product = lax.map(backward, order)
    return gn_product, tangent
```

```python
import functools

import jax
import jax.numpy as jnp
from jax import lax
from jax.experimental import pallas as pl
from jax.experimental.pallas import tpu as pltpu
from jax.sharding import PartitionSpec as P

MESH = pl.DeviceIdType.MESH
F32 = jnp.float32
BF16 = jnp.bfloat16


def spans(widths):
    out, at = [], 0
    for w in widths:
        out.append((at, w))
        at += w
    return out


def dot(a, b):
    return jnp.dot(a, b, preferred_element_type=F32)


class Place:
    def __init__(self):
        self.e = lax.axis_index("ep")
        self.f = lax.axis_index("fsdp")
        self.x = self.f // 2
        self.c = self.f - 2 * self.x
        self.pair = 2 * self.x + 1 - self.c

    def chip(self, off):
        return lax.rem(self.x + off, 4)

    def chunk(self, off, other=False):
        return 2 * self.chip(off) + (1 - self.c if other else self.c)

    def right(self):
        return (self.e, self.chunk(1))

    def left(self):
        return (self.e, self.chunk(3))

    def other(self):
        return (self.e, self.pair)


class AllToAll:
    def __init__(self, at, experts, cap, src, dst, send, recv, pieces):
        self.__dict__.update(locals())

    def start(self, p):
        at, cap = self.at, self.cap
        a, w = self.pieces[p]

        def one(d, carry):
            to = lax.rem(at.e + d, self.experts)
            pltpu.make_async_remote_copy(
                src_ref=self.src.at[pl.ds(pl.multiple_of(to * cap, cap), cap), pl.ds(a, w)],
                dst_ref=self.dst.at[pl.ds(pl.multiple_of(at.e * cap, cap), cap), pl.ds(a, w)],
                send_sem=self.send.at[p],
                recv_sem=self.recv.at[p],
                device_id=(to, at.f),
                device_id_type=MESH,
            ).start()
            return carry

        lax.fori_loop(1, self.experts, one, 0)

    def _all(self, p, sem):
        a, w = self.pieces[p]
        ref = self.src.at[pl.ds(0, (self.experts - 1) * self.cap), pl.ds(a, w)]
        pltpu.make_async_copy(ref, ref, sem.at[p]).wait()

    def wait(self, p):
        self._all(p, self.recv)

    def drain(self, p):
        self._all(p, self.send)


class Gather:
    KINDS = 8

    def __init__(self, at, buf, send, recv, pieces):
        self.__dict__.update(locals())
        self.rows = buf.shape[1]

    def copy(self, p, kind):
        at, half = self.at, self.rows // 2
        a, w = self.pieces[p]
        off = (0, 0, 0, 3, 1, 3, 1, 2)[kind]
        to = (at.other, at.right, at.left, at.right, at.left, at.other, at.other, at.other)[kind]()
        r0, n = {3: (0, half), 4: (half, half)}.get(kind, (0, self.rows))
        ref = self.buf.at[at.chunk(off), pl.ds(r0, n), pl.ds(a, w)]
        return pltpu.make_async_remote_copy(
            src_ref=ref,
            dst_ref=ref,
            send_sem=self.send.at[p, kind],
            recv_sem=self.recv.at[p, kind],
            device_id=to,
            device_id_type=MESH,
        )

    def one(self, p):
        for kind in (1, 2, 0):
            self.copy(p, kind).start()

    def two(self, p):
        self.copy(p, 1).wait_recv()
        self.copy(p, 3).start()
        self.copy(p, 2).wait_recv()
        self.copy(p, 4).start()
        self.copy(p, 5).start()
        self.copy(p, 6).start()

    def three(self, p):
        self.copy(p, 3).wait_recv()
        self.copy(p, 4).wait_recv()
        self.copy(p, 7).start()

    def done(self, p):
        for kind in (0, 5, 6, 7):
            self.copy(p, kind).wait_recv()

    def drain(self, p):
        for kind in range(self.KINDS):
            self.copy(p, kind).wait_send()


def kernel(
    pieces, experts, cap,
    ids_ref, gates_ref, tok_ref, wg_ref, wu_ref, td_ref,
    gn_ref, tan_ref,
    tokv, wgv, wuv, tdv, sel, gsl, comb_hi, comb_lo, send, xbuf, acc_g, acc_u, hid, hid_t,
    psend, precv, rsend, rrecv, fin, ret, wsend, wbuf, gnv,
    load, a_sem, g_send, g_recv, r_send, r_recv, out_sem,
):
    at = Place()
    n = len(pieces)
    toks, chunk = tokv.shape
    rows = experts * cap
    half = rows // 2

    loads = [pltpu.make_async_copy(
        tok_ref.at[:, pl.ds(pl.multiple_of(at.f * chunk, 128), chunk)], tokv, load.at[0])]
    loads += [pltpu.make_async_copy(wg_ref.at[0], wgv, load.at[1]),
              pltpu.make_async_copy(wu_ref.at[0], wuv, load.at[2])]
    loads += [pltpu.make_async_copy(
        td_ref.at[0, :, pl.ds(k * chunk, chunk)], tdv.at[k], load.at[3 + k]) for k in range(8)]
    for copy in loads:
        copy.start()

    barrier = pltpu.get_barrier_semaphore()

    def greet(d, carry):
        pl.semaphore_signal(
            barrier, inc=1, device_id=(lax.rem(at.e + d, experts), at.f), device_id_type=MESH)
        return carry

    lax.fori_loop(1, experts, greet, 0)
    for to in (at.right(), at.left(), at.other()):
        pl.semaphore_signal(barrier, inc=1, device_id=to, device_id_type=MESH)

    lane = lax.broadcasted_iota(jnp.int32, (toks, 128), 1)
    named = [ids_ref[:, k:k + 1] == lane for k in range(ids_ref.shape[1])]
    mask = sum(jnp.where(m, 1.0, 0.0) for m in named)
    gate = sum(jnp.where(m, gates_ref[:, k:k + 1], 0.0) for k, m in enumerate(named))
    mask_t, gate_t = mask.T, gate.T
    earlier = jnp.where(
        lax.broadcasted_iota(jnp.int32, (toks, toks), 0)
        < lax.broadcasted_iota(jnp.int32, (toks, toks), 1), 1.0, 0.0)
    rank_t = dot(mask_t.astype(BF16), earlier.astype(BF16))
    place = lax.broadcasted_iota(jnp.int32, (cap, toks), 0).astype(F32)
    for k in range(experts):
        here = (rank_t[k:k + 1, :] == place) & (mask_t[k:k + 1, :] > 0.5)
        picked = jnp.where(here, gate_t[k:k + 1, :], 0.0)
        sel[k * cap:(k + 1) * cap, :] = jnp.where(here, 1.0, 0.0).astype(BF16)
        gsl[k * cap:(k + 1) * cap, :] = jnp.sum(picked, axis=1, keepdims=True)
        picked_t = picked.T
        hi = picked_t.astype(BF16)
        comb_hi[k] = hi
        comb_lo[k] = (picked_t - hi.astype(F32)).astype(BF16)

    mine = pl.ds(pl.multiple_of(at.e * cap, cap), cap)
    loads[0].wait()
    for a, w in pieces:
        send[:, a:a + w] = dot(sel[...], tokv[:, a:a + w]).astype(BF16)
        xbuf[at.f, mine, a:a + w] = send[mine, a:a + w]
    acc_g[...] = jnp.zeros_like(acc_g)
    acc_u[...] = jnp.zeros_like(acc_u)

    pl.semaphore_wait(barrier, experts - 1 + 3)

    out_a = AllToAll(at, experts, cap, send, xbuf.at[at.f], a_sem.at[0], a_sem.at[1], pieces)
    out_g = Gather(at, xbuf, g_send.at[0], g_recv.at[0], pieces)

    def up(p):
        a, w = pieces[p]

        def tile(m, carry):
            r = pl.ds(pl.multiple_of(m * half, half), half)
            g, u = acc_g[r, :], acc_u[r, :]
            for k in range(8):
                xk = xbuf[k, r, a:a + w]
                g += dot(xk, wgv[k * chunk + a:k * chunk + a + w, :])
                u += dot(xk, wuv[k * chunk + a:k * chunk + a + w, :])
            acc_g[r, :] = g
            acc_u[r, :] = u
            return carry

        lax.fori_loop(0, 2, tile, 0)

    def in_steps(stages):
        for t in range(n + len(stages) - 1):
            for s, stage in enumerate(stages):
                if 0 <= t - s < n:
                    stage(t - s)

    for p in range(n):
        out_a.start(p)

    def x_one(p):
        out_a.wait(p)
        out_g.one(p)

    def x_up(p):
        if p == 0:
            loads[1].wait()
            loads[2].wait()
        out_g.done(p)
        up(p)

    in_steps([x_one, out_g.two, out_g.three, x_up])

    def silu(m, carry):
        r = pl.ds(pl.multiple_of(m * cap, cap), cap)
        g = acc_g[r, :]
        hid[r, :] = (g / (1.0 + jnp.exp(-g)) * acc_u[r, :]).astype(BF16)
        return carry

    lax.fori_loop(0, rows // cap, silu, 0)
    hid_t[...] = hid[...].astype(F32).T.astype(BF16)
    for copy in loads[3:]:
        copy.wait()

    offs = (2, 1, 3, 0)

    def rcopy(p, kind):
        a, w = pieces[p]
        cols = pl.ds(a, w)
        whole, top, low = pl.ds(0, rows), pl.ds(0, half), pl.ds(half, half)
        if kind < 4:
            src, dst, r, to = psend.at[kind], precv.at[kind], whole, at.other()
        else:
            src, dst, r, to = (
                (rsend.at[0], rrecv.at[0], top, at.right()),
                (rsend.at[0], rrecv.at[0], low, at.left()),
                (rsend.at[1], rrecv.at[1], whole, at.right()),
                (rsend.at[2], rrecv.at[2], whole, at.left()),
            )[kind - 4]
        return pltpu.make_async_remote_copy(
            src_ref=src.at[r, cols], dst_ref=dst.at[r, cols],
            send_sem=r_send.at[p, kind], recv_sem=r_recv.at[p, kind],
            device_id=to, device_id_type=MESH)

    def partial(p, j, other, m):
        a, w = pieces[p]
        r = pl.ds(pl.multiple_of(m * half, half), half)
        return r, dot(hid[r, :], tdv[at.chunk(offs[j], other), :, a:a + w])

    def to_pair(p):
        a, w = pieces[p]
        for j in range(4):
            def tile(m, carry):
                r, v = partial(p, j, True, m)
                psend[j, r, a:a + w] = v.astype(BF16)
                return carry

            lax.fori_loop(0, 2, tile, 0)
            rcopy(p, j).start()

    def summed(p, j, m, adds):
        a, w = pieces[p]
        r, v = partial(p, j, False, m)
        v += precv[j, r, a:a + w].astype(F32)
        for k in adds:
            v += rrecv[k, r, a:a + w].astype(F32)
        return r, v.astype(BF16)

    def far(p):
        a, w = pieces[p]
        rcopy(p, 0).wait_recv()
        for m in range(2):
            r, v = summed(p, 0, m, ())
            rsend[0, r, a:a + w] = v
            rcopy(p, 4 + m).start()

    def near(p):
        a, w = pieces[p]
        for j in (1, 2):
            rcopy(p, j).wait_recv()
            rcopy(p, 3 + j).wait_recv()
            for m in range(2):
                r, v = summed(p, j, m, (0,) if m == j - 1 else ())
                rsend[j, r, a:a + w] = v
            rcopy(p, 5 + j).start()

    back = AllToAll(at, experts, cap, fin, ret, a_sem.at[2], a_sem.at[3], pieces)

    def home(p):
        a, w = pieces[p]
        for kind in (3, 6, 7):
            rcopy(p, kind).wait_recv()
        for m in range(2):
            r, v = summed(p, 3, m, (1, 2))
            fin[r, a:a + w] = v
        back.start(p)
        ret[mine, a:a + w] = fin[mine, a:a + w]

    out_w = AllToAll(at, experts, cap, wsend, wbuf.at[at.f], a_sem.at[4], a_sem.at[5], pieces)
    out_v = Gather(at, wbuf, g_send.at[1], g_recv.at[1], pieces)

    def combine(p):
        a, w = pieces[p]
        back.wait(p)
        total = jnp.zeros((toks, w), F32)
        for k in range(experts):
            got = ret[k * cap:(k + 1) * cap, a:a + w]
            total += dot(comb_hi[k], got) + dot(comb_lo[k], got)
        tangent = total.astype(BF16)
        tan_ref[:, a:a + w] = tangent
        for m in range(2):
            r = pl.ds(m * half, half)
            wsend[r, a:a + w] = (dot(sel[r, :], tangent) * gsl[r, :]).astype(BF16)
        out_w.start(p)
        wbuf[at.f, mine, a:a + w] = wsend[mine, a:a + w]

    def w_one(p):
        out_w.wait(p)
        out_v.one(p)

    def out_copy(p, k):
        a, w = pieces[p]
        return pltpu.make_async_copy(
            gnv.at[k, :, pl.ds(a, w)], gn_ref.at[0, :, pl.ds(k * chunk + a, w)], out_sem.at[p, k])

    def product(p):
        a, w = pieces[p]
        out_v.done(p)
        for k in range(8):
            gnv[k, :, a:a + w] = dot(hid_t[...], wbuf[k, :, a:a + w])
            out_copy(p, k).start()

    in_steps([to_pair, far, near, home, combine, w_one, out_v.two, out_v.three, product])

    for p in range(n):
        for moved in (out_a, back, out_w, out_g, out_v):
            moved.drain(p)
        for kind in range(8):
            rcopy(p, kind).wait_send()
        for k in range(8):
            out_copy(p, k).wait()


def on_device(widths, cap, tokens, w_gate, w_up, tangent_down, gates, expert_ids):
    experts = lax.axis_size("ep")
    toks, width = tokens.shape
    chunk = width // 8
    hidden = w_gate.shape[2]
    rows = experts * cap
    pieces = spans(widths)
    n = len(pieces)
    vmem, anywhere = pl.BlockSpec(memory_space=pltpu.VMEM), pl.BlockSpec(memory_space=pl.ANY)
    gn, tangent = pl.pallas_call(
        functools.partial(kernel, pieces, experts, cap),
        out_shape=(
            jax.ShapeDtypeStruct((1, hidden, width), F32),
            jax.ShapeDtypeStruct((toks, chunk), BF16),
        ),
        in_specs=[vmem, vmem, anywhere, anywhere, anywhere, anywhere],
        out_specs=(anywhere, vmem),
        scratch_shapes=[
            pltpu.VMEM((toks, chunk), BF16),
            pltpu.VMEM((width, hidden), BF16),
            pltpu.VMEM((width, hidden), BF16),
            pltpu.VMEM((8, hidden, chunk), BF16),
            pltpu.VMEM((rows, toks), BF16),
            pltpu.VMEM((rows, 1), F32),
            pltpu.VMEM((experts, toks, cap), BF16),
            pltpu.VMEM((experts, toks, cap), BF16),
            pltpu.VMEM((rows, chunk), BF16),
            pltpu.VMEM((8, rows, chunk), BF16),
            pltpu.VMEM((rows, hidden), F32),
            pltpu.VMEM((rows, hidden), F32),
            pltpu.VMEM((rows, hidden), BF16),
            pltpu.VMEM((hidden, rows), BF16),
            pltpu.VMEM((4, rows, chunk), BF16),
            pltpu.VMEM((4, rows, chunk), BF16),
            pltpu.VMEM((3, rows, chunk), BF16),
            pltpu.VMEM((3, rows, chunk), BF16),
            pltpu.VMEM((rows, chunk), BF16),
            pltpu.VMEM((rows, chunk), BF16),
            pltpu.VMEM((rows, chunk), BF16),
            pltpu.VMEM((8, rows, chunk), BF16),
            pltpu.VMEM((8, hidden, chunk), F32),
            pltpu.SemaphoreType.DMA((11,)),
            pltpu.SemaphoreType.DMA((6, n)),
            pltpu.SemaphoreType.DMA((2, n, 8)),
            pltpu.SemaphoreType.DMA((2, n, 8)),
            pltpu.SemaphoreType.DMA((n, 8)),
            pltpu.SemaphoreType.DMA((n, 8)),
            pltpu.SemaphoreType.DMA((n, 8)),
        ],
        compiler_params=pltpu.CompilerParams(
            collective_id=0, has_side_effects=True, vmem_limit_bytes=60 * 2**20),
    )(expert_ids, gates, tokens, w_gate, w_up, tangent_down)
    return gn, tangent


def solution(mesh, widths=(256, 256, 384), cap=32):
    in_specs = (
        P("ep", None),
        P("ep", None, "fsdp"),
        P("ep", None, "fsdp"),
        P("ep", "fsdp", None),
        P("ep", None),
        P("ep", None),
    )
    out_specs = (P("ep", "fsdp", None), P("ep", "fsdp"))
    return jax.shard_map(
        functools.partial(on_device, widths, cap),
        mesh=mesh, in_specs=in_specs, out_specs=out_specs, check_vma=False,
    )
```

```python
import functools

import jax
import jax.numpy as jnp
from jax import lax
from jax.experimental import pallas as pl
from jax.experimental.pallas import tpu as pltpu
from jax.sharding import PartitionSpec as P

MESH = pl.DeviceIdType.MESH
F32 = jnp.float32
BF16 = jnp.bfloat16


def spans(widths):
    out, at = [], 0
    for w in widths:
        out.append((at, w))
        at += w
    return out


def dot(a, b):
    return jnp.dot(a, b, preferred_element_type=F32)


def cbh(k):
    return k % 2, k // 2 % 2, k // 4


class Place:
    def __init__(self):
        self.e = lax.axis_index("ep")
        self.f = lax.axis_index("fsdp")
        self.x = self.f // 2
        self.c = self.f - 2 * self.x
        self.h = self.x // 2
        self.b = self.x - 2 * self.h

    def chip(self, off):
        return lax.rem(self.x + off, 4)

    def chunk(self, off, other=False):
        return 2 * self.chip(off) + (1 - self.c if other else self.c)

    def to(self, off):
        return (self.e, self.chunk(off))

    def pair(self):
        return (self.e, self.chunk(0, True))


class AllToAll:
    def __init__(self, at, experts, cap, src, dst, send, recv, pieces):
        self.__dict__.update(locals())

    def start(self, p):
        at, cap = self.at, self.cap
        a, w = self.pieces[p]

        def one(d, carry):
            to = lax.rem(at.e + d, self.experts)
            pltpu.make_async_remote_copy(
                src_ref=self.src.at[:, pl.ds(pl.multiple_of(to * cap, cap), cap), pl.ds(a, w)],
                dst_ref=self.dst.at[:, pl.ds(pl.multiple_of(at.e * cap, cap), cap), pl.ds(a, w)],
                send_sem=self.send.at[p],
                recv_sem=self.recv.at[p],
                device_id=(to, at.f),
                device_id_type=MESH,
            ).start()
            return carry

        lax.fori_loop(1, self.experts, one, 0)

    def _all(self, p, sem):
        a, w = self.pieces[p]
        ref = self.src.at[:, pl.ds(0, (self.experts - 1) * self.cap), pl.ds(a, w)]
        pltpu.make_async_copy(ref, ref, sem.at[p]).wait()

    def wait(self, p):
        self._all(p, self.recv)

    def drain(self, p):
        self._all(p, self.send)


class Gather:
    KINDS = 5

    def __init__(self, at, buf, send, recv, pieces):
        self.__dict__.update(locals())

    def copy(self, p, kind):
        at = self.at
        a, w = self.pieces[p]
        cols = pl.ds(a, w)
        if kind == 2:
            ref = self.buf.at[at.c, at.b, :, :, cols]
        elif kind < 2:
            ref = self.buf.at[at.c, at.b, at.h, :, cols]
        else:
            ref = self.buf.at[at.c, 1 - at.b, at.chip(3 if kind == 3 else 1) // 2, :, cols]
        to = (at.to(1), at.to(3), at.pair(), at.pair(), at.pair())[kind]
        return pltpu.make_async_remote_copy(
            src_ref=ref,
            dst_ref=ref,
            send_sem=self.send.at[p, kind],
            recv_sem=self.recv.at[p, kind],
            device_id=to,
            device_id_type=MESH,
        )

    def one(self, p):
        for kind in (0, 1, 2):
            self.copy(p, kind).start()

    def two(self, p):
        for kind in (0, 1):
            self.copy(p, kind).wait_recv()
            self.copy(p, kind + 3).start()

    def done(self, p):
        for kind in (2, 3, 4):
            self.copy(p, kind).wait_recv()

    def drain(self, p):
        for kind in range(self.KINDS):
            self.copy(p, kind).wait_send()


def kernel(
    xpieces, pieces, experts, cap, upto,
    ids_ref, gates_ref, tok_ref, wg_ref, wu_ref, td_ref,
    gn_ref, tan_ref,
    tokv, wgv, wuv, tdv, sel, selg, gsl, comb_hi, comb_lo, send, xbuf, acc_g, acc_u, hid, hid_t,
    psend, precv, rsend, rrecv, fin, ret, tsend, trecv, wsend, wbuf, gnv,
    load, x_sem, a_sem, xg_send, xg_recv, g_send, g_recv, r_send, r_recv, out_sem,
):
    at = Place()
    nx, n = len(xpieces), len(pieces)
    toks, chunk = tokv.shape[1:]
    rows = experts * cap
    half = rows // 2
    drains = []

    loads = [pltpu.make_async_copy(
        tok_ref.at[:, pl.ds(pl.multiple_of((4 * h + 2 * at.b + at.c) * chunk, 128), chunk)],
        tokv.at[h], load.at[h]) for h in range(2)]
    loads += [pltpu.make_async_copy(wg_ref.at[0], wgv, load.at[2]),
              pltpu.make_async_copy(wu_ref.at[0], wuv, load.at[3])]
    loads += [pltpu.make_async_copy(
        td_ref.at[0, :, pl.ds(k * chunk, chunk)], tdv.at[k], load.at[4 + k]) for k in range(8)]
    for copy in loads:
        copy.start()

    barrier = pltpu.get_barrier_semaphore()

    def greet(d, carry):
        pl.semaphore_signal(
            barrier, inc=1, device_id=(lax.rem(at.e + d, experts), at.f), device_id_type=MESH)
        return carry

    lax.fori_loop(1, experts, greet, 0)
    for to in (at.to(1), at.to(3), at.to(2), at.pair()):
        pl.semaphore_signal(barrier, inc=1, device_id=to, device_id_type=MESH)

    expert = lax.broadcasted_iota(jnp.int32, (experts, toks), 0)
    named = [ids_ref[k:k + 1, :] == expert for k in range(ids_ref.shape[0])]
    mask_t = sum(jnp.where(m, 1.0, 0.0) for m in named)
    gate_t = sum(jnp.where(m, gates_ref[k:k + 1, :], 0.0) for k, m in enumerate(named))
    earlier = jnp.where(
        lax.broadcasted_iota(jnp.int32, (toks, toks), 0)
        < lax.broadcasted_iota(jnp.int32, (toks, toks), 1), 1.0, 0.0)
    rank_t = dot(mask_t.astype(BF16), earlier.astype(BF16))
    place = lax.broadcasted_iota(jnp.int32, (cap, toks), 0).astype(F32)
    for k in range(experts):
        here = (rank_t[k:k + 1, :] == place) & (mask_t[k:k + 1, :] > 0.5)
        picked = jnp.where(here, gate_t[k:k + 1, :], 0.0)
        sel[k * cap:(k + 1) * cap, :] = jnp.where(here, 1.0, 0.0).astype(BF16)
        selg[k * cap:(k + 1) * cap, :] = picked
        gsl[k * cap:(k + 1) * cap, :] = jnp.sum(picked, axis=1, keepdims=True)

    mine = pl.ds(pl.multiple_of(at.e * cap, cap), cap)
    loads[0].wait()
    loads[1].wait()
    for a, w in xpieces:
        for h in range(2):
            send[h, :, a:a + w] = dot(sel[...], tokv[h, :, a:a + w]).astype(BF16)
            xbuf[at.c, at.b, h, mine, a:a + w] = send[h, mine, a:a + w]

    pl.semaphore_wait(barrier, experts - 1 + 4)

    out_a = AllToAll(
        at, experts, cap, send, xbuf.at[at.c, at.b], x_sem.at[0], x_sem.at[1], xpieces)
    out_g = Gather(at, xbuf, xg_send, xg_recv, xpieces)
    for p in range(nx):
        out_a.start(p)

    acc_g[...] = jnp.zeros_like(acc_g)
    acc_u[...] = jnp.zeros_like(acc_u)
    comb = selg[...].T
    hi = comb.astype(BF16)
    comb_hi[...] = hi
    comb_lo[...] = (comb - hi.astype(F32)).astype(BF16)

    def up(p):
        a, w = xpieces[p]

        def tile(m, carry):
            r = pl.ds(pl.multiple_of(m * half, half), half)
            g, u = acc_g[r, :], acc_u[r, :]
            for k in range(8):
                xk = xbuf[*cbh(k), r, a:a + w]
                g += dot(xk, wgv[k * chunk + a:k * chunk + a + w, :])
                u += dot(xk, wuv[k * chunk + a:k * chunk + a + w, :])
            acc_g[r, :] = g
            acc_u[r, :] = u
            return carry

        lax.fori_loop(0, 2, tile, 0)

    def in_steps(n, stages):
        for t in range(n + len(stages) - 1):
            for s, stage in enumerate(stages):
                if 0 <= t - s < n:
                    stage(t - s)

    def x_one(p):
        out_a.wait(p)
        out_g.one(p)

    def x_up(p):
        if p == 0:
            loads[2].wait()
            loads[3].wait()
        out_g.done(p)
        up(p)

    in_steps(nx, [x_one, out_g.two, x_up])
    drains += [(out_a.drain, nx), (out_g.drain, nx)]

    def silu(m, carry):
        r = pl.ds(pl.multiple_of(m * cap, cap), cap)
        g = acc_g[r, :]
        hid[r, :] = (g / (1.0 + jnp.exp(-g)) * acc_u[r, :]).astype(BF16)
        return carry

    lax.fori_loop(0, rows // cap, silu, 0)
    for copy in loads[4:]:
        copy.wait()

    offs = (1, 3, 2, 0)

    def rcopy(p, kind):
        a, w = pieces[p]
        if kind < 4:
            src, dst, to = psend.at[kind], precv.at[kind], at.pair()
        else:
            src, dst, to = rsend.at[kind - 4], rrecv.at[kind - 4], at.to(1 if kind == 4 else 3)
        return pltpu.make_async_remote_copy(
            src_ref=src.at[:, pl.ds(a, w)], dst_ref=dst.at[:, pl.ds(a, w)],
            send_sem=r_send.at[p, kind], recv_sem=r_recv.at[p, kind],
            device_id=to, device_id_type=MESH)

    def r_drain(p):
        for kind in range(6):
            rcopy(p, kind).wait_send()

    def partial(p, j, other, m):
        a, w = pieces[p]
        r = pl.ds(pl.multiple_of(m * half, half), half)
        return r, dot(hid[r, :], tdv[at.chunk(offs[j], other), :, a:a + w])

    def to_pair(p):
        a, w = pieces[p]
        for j in range(4):
            def tile(m, carry):
                r, v = partial(p, j, True, m)
                psend[j, r, a:a + w] = v.astype(BF16)
                return carry

            lax.fori_loop(0, 2, tile, 0)
            rcopy(p, j).start()

    def summed(p, j, adds, store):
        a, w = pieces[p]
        rcopy(p, j).wait_recv()

        def tile(m, carry):
            r, v = partial(p, j, False, m)
            v += precv[j, r, a:a + w].astype(F32)
            for k in adds:
                v += rrecv[k, r, a:a + w].astype(F32)
            store(r, v.astype(BF16))
            return carry

        lax.fori_loop(0, 2, tile, 0)

    def near(p):
        a, w = pieces[p]
        for j in (0, 1):
            def store(r, v):
                rsend[j, r, a:a + w] = v

            summed(p, j, (), store)
            rcopy(p, 4 + j).start()

    back = AllToAll(at, experts, cap, fin, ret, a_sem.at[0], a_sem.at[1], pieces)

    def home(p):
        a, w = pieces[p]

        def store_far(r, v):
            fin[1 - at.h, r, a:a + w] = v

        def store_own(r, v):
            fin[at.h, r, a:a + w] = v

        summed(p, 2, (), store_far)
        rcopy(p, 4).wait_recv()
        rcopy(p, 5).wait_recv()
        summed(p, 3, (0, 1), store_own)
        back.start(p)
        for h in range(2):
            ret[h, mine, a:a + w] = fin[h, mine, a:a + w]

    def tcopy(p):
        a, w = pieces[p]
        return pltpu.make_async_remote_copy(
            src_ref=tsend.at[:, :, pl.ds(a, w)], dst_ref=trecv.at[:, :, pl.ds(a, w)],
            send_sem=r_send.at[p, 6], recv_sem=r_recv.at[p, 6],
            device_id=at.to(2), device_id_type=MESH)

    def combine(p):
        a, w = pieces[p]
        back.wait(p)
        for h in range(2):
            got = ret[h, :, a:a + w]
            tsend[h, :, a:a + w] = (dot(comb_hi[...], got) + dot(comb_lo[...], got)).astype(BF16)
        tcopy(p).start()

    out_w = AllToAll(
        at, experts, cap, wsend, wbuf.at[at.c, at.b], a_sem.at[2], a_sem.at[3], pieces)
    out_v = Gather(at, wbuf, g_send, g_recv, pieces)

    def weigh(p):
        a, w = pieces[p]
        tcopy(p).wait_recv()
        both = []
        for h in range(2):
            total = tsend[h, :, a:a + w].astype(F32) + trecv[h, :, a:a + w].astype(F32)
            both.append(total.astype(BF16))
            for m in range(2):
                r = pl.ds(m * half, half)
                wsend[h, r, a:a + w] = (dot(sel[r, :], both[h]) * gsl[r, :]).astype(BF16)
        out_w.start(p)
        tan_ref[:, a:a + w] = jnp.where(at.h == 0, both[0], both[1])
        for h in range(2):
            wbuf[at.c, at.b, h, mine, a:a + w] = wsend[h, mine, a:a + w]

    def w_one(p):
        out_w.wait(p)
        out_v.one(p)

    def out_copy(p, k):
        a, w = pieces[p]
        return pltpu.make_async_copy(
            gnv.at[k, :, pl.ds(a, w)], gn_ref.at[0, :, pl.ds(k * chunk + a, w)], out_sem.at[p, k])

    def out_drain(p):
        for k in range(8):
            out_copy(p, k).wait()

    def product(p):
        a, w = pieces[p]
        if p == 0:
            hid_t[...] = hid[...].astype(F32).T.astype(BF16)
        out_v.done(p)
        for k in range(8):
            gnv[k, :, a:a + w] = dot(hid_t[...], wbuf[*cbh(k), :, a:a + w])
            out_copy(p, k).start()

    def t_drain(p):
        tcopy(p).wait_send()

    stages = [to_pair, near, home, combine, weigh, w_one, out_v.two, product]
    if upto is not None:
        stages = stages[:upto]
    if stages:
        in_steps(n, stages)
    ends = {1: r_drain, 3: back.drain, 4: t_drain, 5: out_w.drain, 7: out_v.drain, 8: out_drain}
    drains += [(end, n) for stage, end in ends.items() if len(stages) >= stage]
    for drain, count in drains:
        for p in range(count):
            drain(p)


def on_device(xwidths, widths, cap, upto, tokens, w_gate, w_up, tangent_down, gates, expert_ids):
    experts = lax.axis_size("ep")
    toks, width = tokens.shape
    chunk = width // 8
    hidden = w_gate.shape[2]
    rows = experts * cap
    xpieces, pieces = spans(xwidths), spans(widths)
    nx, n = len(xpieces), len(pieces)
    vmem, anywhere = pl.BlockSpec(memory_space=pltpu.VMEM), pl.BlockSpec(memory_space=pl.ANY)
    gn, tangent = pl.pallas_call(
        functools.partial(kernel, xpieces, pieces, experts, cap, upto),
        out_shape=(
            jax.ShapeDtypeStruct((1, hidden, width), F32),
            jax.ShapeDtypeStruct((toks, chunk), BF16),
        ),
        in_specs=[vmem, vmem, anywhere, anywhere, anywhere, anywhere],
        out_specs=(anywhere, vmem),
        scratch_shapes=[
            pltpu.VMEM((2, toks, chunk), BF16),
            pltpu.VMEM((width, hidden), BF16),
            pltpu.VMEM((width, hidden), BF16),
            pltpu.VMEM((8, hidden, chunk), BF16),
            pltpu.VMEM((rows, toks), BF16),
            pltpu.VMEM((rows, toks), F32),
            pltpu.VMEM((rows, 1), F32),
            pltpu.VMEM((toks, rows), BF16),
            pltpu.VMEM((toks, rows), BF16),
            pltpu.VMEM((2, rows, chunk), BF16),
            pltpu.VMEM((2, 2, 2, rows, chunk), BF16),
            pltpu.VMEM((rows, hidden), F32),
            pltpu.VMEM((rows, hidden), F32),
            pltpu.VMEM((rows, hidden), BF16),
            pltpu.VMEM((hidden, rows), BF16),
            pltpu.VMEM((4, rows, chunk), BF16),
            pltpu.VMEM((4, rows, chunk), BF16),
            pltpu.VMEM((2, rows, chunk), BF16),
            pltpu.VMEM((2, rows, chunk), BF16),
            pltpu.VMEM((2, rows, chunk), BF16),
            pltpu.VMEM((2, rows, chunk), BF16),
            pltpu.VMEM((2, toks, chunk), BF16),
            pltpu.VMEM((2, toks, chunk), BF16),
            pltpu.VMEM((2, rows, chunk), BF16),
            pltpu.VMEM((2, 2, 2, rows, chunk), BF16),
            pltpu.VMEM((8, hidden, chunk), F32),
            pltpu.SemaphoreType.DMA((12,)),
            pltpu.SemaphoreType.DMA((2, nx)),
            pltpu.SemaphoreType.DMA((4, n)),
            pltpu.SemaphoreType.DMA((nx, 5)),
            pltpu.SemaphoreType.DMA((nx, 5)),
            pltpu.SemaphoreType.DMA((n, 5)),
            pltpu.SemaphoreType.DMA((n, 5)),
            pltpu.SemaphoreType.DMA((n, 7)),
            pltpu.SemaphoreType.DMA((n, 7)),
            pltpu.SemaphoreType.DMA((n, 8)),
        ],
        compiler_params=pltpu.CompilerParams(
            collective_id=0, has_side_effects=True, vmem_limit_bytes=60 * 2**20),
    )(expert_ids.T, gates.T, tokens, w_gate, w_up, tangent_down)
    return gn, tangent


def solution(mesh, xwidths=(128,) * 7, widths=(128,) * 7, cap=32, upto=None):
    in_specs = (
        P("ep", None),
        P("ep", None, "fsdp"),
        P("ep", None, "fsdp"),
        P("ep", "fsdp", None),
        P("ep", None),
        P("ep", None),
    )
    out_specs = (P("ep", "fsdp", None), P("ep", "fsdp"))
    return jax.shard_map(
        functools.partial(on_device, xwidths, widths, cap, upto),
        mesh=mesh, in_specs=in_specs, out_specs=out_specs, check_vma=False,
    )
```

```python
import functools

import jax
import jax.numpy as jnp
from jax import lax
from jax.experimental import pallas as pl
from jax.experimental.pallas import tpu as pltpu
from jax.sharding import PartitionSpec as P

MESH = pl.DeviceIdType.MESH
F32 = jnp.float32
BF16 = jnp.bfloat16


def spans(widths):
    out, at = [], 0
    for w in widths:
        out.append((at, w))
        at += w
    return out


def dot(a, b):
    return jnp.dot(a, b, preferred_element_type=F32)


def wide(blocks):
    return jnp.concatenate(blocks, axis=1)


def cbh(k):
    return k % 2, k // 2 % 2, k // 4


class Place:
    def __init__(self):
        self.e = lax.axis_index("ep")
        self.f = lax.axis_index("fsdp")
        self.x = self.f // 2
        self.c = self.f - 2 * self.x
        self.h = self.x // 2
        self.b = self.x - 2 * self.h

    def chip(self, off):
        return lax.rem(self.x + off, 4)

    def chunk(self, off, other=False):
        return 2 * self.chip(off) + (1 - self.c if other else self.c)

    def to(self, off):
        return (self.e, self.chunk(off))

    def pair(self):
        return (self.e, self.chunk(0, True))


class AllToAll:
    def __init__(self, at, experts, cap, src, dst, send, recv):
        self.__dict__.update(locals())

    def start(self, i, groups, a, w):
        at, cap = self.at, self.cap

        def one(d, carry):
            to = lax.rem(at.e + d, self.experts)
            pltpu.make_async_remote_copy(
                src_ref=self.src.at[
                    :, groups, pl.ds(pl.multiple_of(to * cap, cap), cap), pl.ds(a, w)],
                dst_ref=self.dst.at[
                    :, groups, pl.ds(pl.multiple_of(at.e * cap, cap), cap), pl.ds(a, w)],
                send_sem=self.send.at[i],
                recv_sem=self.recv.at[i],
                device_id=(to, at.f),
                device_id_type=MESH,
            ).start()
            return carry

        lax.fori_loop(1, self.experts, one, 0)

    def _all(self, sem, i, groups, a, w):
        ref = self.src.at[:, groups, pl.ds(0, (self.experts - 1) * self.cap), pl.ds(a, w)]
        pltpu.make_async_copy(ref, ref, sem.at[i]).wait()

    def wait(self, *piece):
        self._all(self.recv, *piece)

    def drain(self, *piece):
        self._all(self.send, *piece)


class Gather:
    KINDS = 5

    def __init__(self, at, buf, send, recv):
        self.__dict__.update(locals())

    def copy(self, kind, i, groups, a, w):
        at = self.at
        cols = pl.ds(a, w)
        if kind == 2:
            ref = self.buf.at[at.c, at.b, :, groups, :, cols]
        elif kind < 2:
            ref = self.buf.at[at.c, at.b, at.h, groups, :, cols]
        else:
            ref = self.buf.at[at.c, 1 - at.b, at.chip(3 if kind == 3 else 1) // 2, groups, :, cols]
        to = (at.to(1), at.to(3), at.pair(), at.pair(), at.pair())[kind]
        return pltpu.make_async_remote_copy(
            src_ref=ref,
            dst_ref=ref,
            send_sem=self.send.at[i, kind],
            recv_sem=self.recv.at[i, kind],
            device_id=to,
            device_id_type=MESH,
        )

    def one(self, *piece):
        for kind in (0, 1, 2):
            self.copy(kind, *piece).start()

    def two(self, *piece):
        for kind in (0, 1):
            self.copy(kind, *piece).wait_recv()
            self.copy(kind + 3, *piece).start()

    def done(self, *piece):
        for kind in (2, 3, 4):
            self.copy(kind, *piece).wait_recv()

    def drain(self, *piece):
        for kind in range(self.KINDS):
            self.copy(kind, *piece).wait_send()


def plan(dwidths, rwidths):
    nd, nr = len(dwidths), len(rwidths)
    wd, wr = [w / 896 for w in dwidths], [w / 896 for w in rwidths]
    steps = {}
    for g in range(2):
        for p in range(nd):
            w, i = wd[p], g * nd + p
            steps["a", g, p] = (i, 1.2 * w, [], [("yz", 10 * w)])
            steps["1", g, p] = (i, 0.1, [("a", g, p)], [("x", 10 * w), ("pair", 2 * w)])
            steps["2", g, p] = (i, 0.1, [("1", g, p)], [("pair", 2 * w)])
            steps["u", g, p] = (90 + i, 2.4 * w, [("2", g, p)], [])
        steps["s", g, 0] = (100, 0.6, [("u", g, p) for p in range(nd)], [])
        for p in range(nr):
            w, i = wr[p], 20 + g * nr + p
            steps["t", g, p] = (i, 1.4 * w, [("s", g, 0)], [("pair", 4 * w)])
            steps["n", g, p] = (i, 1.2 * w, [("t", g, p)], [("x", 10 * w)])
            steps["h", g, p] = (i, 1.4 * w, [("n", g, p)], [("yz", 10 * w)])
    for p in range(nr):
        w, i = wr[p], 40 + p
        steps["c", 0, p] = (i, 1.4 * w, [("h", 0, p), ("h", 1, p)], [("x", 10 * w)])
        steps["w", 0, p] = (i, 1.6 * w, [("c", 0, p)], [("yz", 20 * w)])
        steps["3", 0, p] = (i, 0.1, [("w", 0, p)], [("x", 20 * w), ("pair", 4 * w)])
        steps["4", 0, p] = (i, 0.1, [("3", 0, p)], [("pair", 4 * w)])
        steps["p", 0, p] = (200 + i, 2.4 * w, [("4", 0, p)], [])
    delay = {"x": 2.5, "yz": 3.2, "pair": 2.0}
    now, free, there, order = 0.0, {"x": 0.0, "yz": 0.0, "pair": 0.0}, {}, []
    while len(order) < len(steps):
        left = [s for s in steps if s not in there and all(q in there for q in steps[s][2])]
        at = {s: max([there[q] for q in steps[s][2]], default=0.0) for s in left}
        ready = [s for s in left if at[s] <= now]
        if not ready:
            now = min(at.values())
            continue
        step = min(ready, key=lambda s: (steps[s][0], s))
        now += steps[step][1]
        there[step] = now
        for link, time in steps[step][3]:
            free[link] = max(free[link], now) + time
            there[step] = max(there[step], free[link] + delay[link])
        order.append(step)
    return order, now


def kernel(
    dwidths, rwidths, experts, cap, upto,
    ids_ref, gates_ref, tok_ref, wg_ref, wu_ref, td_ref,
    gn_ref, tan_ref,
    tokv, wgv, wuv, tdv, sel, selg, gsl, comb_hi, comb_lo, send, xbuf, acc_g, acc_u, hid, hid_t,
    psend, precv, rsend, rrecv, fin, ret, tsend, trecv, wsend, wbuf,
    load, x_sem, h_sem, w_sem, xg_send, xg_recv, g_send, g_recv, r_send, r_recv, t_sem,
):
    at = Place()
    dspans, rspans = spans(dwidths), spans(rwidths)
    nd, nr = len(dspans), len(rspans)
    toks, chunk = tokv.shape[1:]
    half = experts * cap
    ranks = 2 * cap
    both = slice(None)

    loads = [pltpu.make_async_copy(
        tok_ref.at[:, pl.ds(pl.multiple_of((4 * h + 2 * at.b + at.c) * chunk, 128), chunk)],
        tokv.at[h], load.at[h]) for h in range(2)]
    loads += [pltpu.make_async_copy(wg_ref.at[0], wgv, load.at[2]),
              pltpu.make_async_copy(wu_ref.at[0], wuv, load.at[3])]
    loads += [pltpu.make_async_copy(
        td_ref.at[0, :, pl.ds(k * chunk, chunk)], tdv.at[k], load.at[4 + k]) for k in range(8)]
    for copy in loads:
        copy.start()

    barrier = pltpu.get_barrier_semaphore()

    def greet(d, carry):
        pl.semaphore_signal(
            barrier, inc=1, device_id=(lax.rem(at.e + d, experts), at.f), device_id_type=MESH)
        return carry

    lax.fori_loop(1, experts, greet, 0)
    for to in (at.to(1), at.to(3), at.to(2), at.pair()):
        pl.semaphore_signal(barrier, inc=1, device_id=to, device_id_type=MESH)

    expert = lax.broadcasted_iota(jnp.int32, (experts, toks), 0)
    named = [ids_ref[k:k + 1, :] == expert for k in range(ids_ref.shape[0])]
    mask_t = sum(jnp.where(m, 1.0, 0.0) for m in named)
    gate_t = sum(jnp.where(m, gates_ref[k:k + 1, :], 0.0) for k, m in enumerate(named))
    earlier = jnp.where(
        lax.broadcasted_iota(jnp.int32, (toks, toks), 0)
        < lax.broadcasted_iota(jnp.int32, (toks, toks), 1), 1.0, 0.0)
    rank_t = dot(mask_t.astype(BF16), earlier.astype(BF16))
    place = lax.broadcasted_iota(jnp.int32, (ranks, toks), 0).astype(F32)
    for k in range(experts):
        here = (rank_t[k:k + 1, :] == place) & (mask_t[k:k + 1, :] > 0.5)
        picked = jnp.where(here, gate_t[k:k + 1, :], 0.0)
        one = jnp.where(here, 1.0, 0.0).astype(BF16)
        total = jnp.sum(picked, axis=1, keepdims=True)
        for g in range(2):
            r, part = slice(k * cap, (k + 1) * cap), slice(g * cap, (g + 1) * cap)
            sel[g, r, :] = one[part]
            selg[g, r, :] = picked[part]
            gsl[g, r, :] = total[part]

    mine = pl.ds(pl.multiple_of(at.e * cap, cap), cap)
    out_a = AllToAll(at, experts, cap, send, xbuf.at[at.c, at.b], x_sem.at[0], x_sem.at[1])
    out_g = Gather(at, xbuf, xg_send, xg_recv)
    back = AllToAll(at, experts, cap, fin, ret, h_sem.at[0], h_sem.at[1])
    out_w = AllToAll(at, experts, cap, wsend, wbuf.at[at.c, at.b], w_sem.at[0], w_sem.at[1])
    out_v = Gather(at, wbuf, g_send, g_recv)

    def dpiece(g, p):
        return g * nd + p, pl.ds(g, 1), *dspans[p]

    def rpiece(g, p):
        return g * nr + p, pl.ds(g, 1), *rspans[p]

    def wpiece(p):
        return p, both, *rspans[p]

    def choose(g, p):
        a, w = dspans[p]
        rows = dot(sel[g], wide([tokv[h, :, a:a + w] for h in range(2)])).astype(BF16)
        for h in range(2):
            send[h, g, :, a:a + w] = rows[:, h * w:(h + 1) * w]
        out_a.start(*dpiece(g, p))
        for h in range(2):
            xbuf[at.c, at.b, h, g, mine, a:a + w] = send[h, g, mine, a:a + w]

    def d_one(g, p):
        out_a.wait(*dpiece(g, p))
        out_g.one(*dpiece(g, p))

    def d_two(g, p):
        out_g.two(*dpiece(g, p))

    def up(g, p):
        a, w = dspans[p]
        if (g, p) == (0, 0):
            loads[2].wait()
            loads[3].wait()
        out_g.done(*dpiece(g, p))
        for acc, weights in ((acc_g, wgv), (acc_u, wuv)):
            total = None if p == 0 else acc[g]
            for k in range(0, 8, 2):
                c, b, h = cbh(k)
                part = dot(
                    wide([xbuf[c, b, h, g, :, a:a + w] for c in range(2)]),
                    jnp.concatenate([
                        weights[q * chunk + a:q * chunk + a + w, :] for q in (k, k + 1)], axis=0))
                total = part if total is None else total + part
            acc[g] = total

    def silu(g, _):
        def tile(m, carry):
            r = pl.ds(pl.multiple_of(m * ranks, ranks), ranks)
            v = acc_g[g, r, :]
            hid[g, r, :] = (v / (1.0 + jnp.exp(-v)) * acc_u[g, r, :]).astype(BF16)
            return carry

        lax.fori_loop(0, half // ranks, tile, 0)
        hid_t[g] = hid[g].astype(F32).T.astype(BF16)
        if g == 0:
            for copy in loads[4:]:
                copy.wait()

    offs = (1, 3, 2, 0)

    def rcopy(kind, g, p):
        a, w = rspans[p]
        if kind < 4:
            src, dst, to = psend.at[kind], precv.at[kind], at.pair()
        else:
            src, dst, to = rsend.at[kind - 4], rrecv.at[kind - 4], at.to(1 if kind == 4 else 3)
        return pltpu.make_async_remote_copy(
            src_ref=src.at[g, :, pl.ds(a, w)], dst_ref=dst.at[g, :, pl.ds(a, w)],
            send_sem=r_send.at[g * nr + p, kind], recv_sem=r_recv.at[g * nr + p, kind],
            device_id=to, device_id_type=MESH)

    def partial(g, p, js, other):
        a, w = rspans[p]
        v = dot(hid[g], wide([tdv[at.chunk(offs[j], other), :, a:a + w] for j in js]))
        return [v[:, i * w:(i + 1) * w] for i in range(len(js))]

    def to_pair(g, p):
        a, w = rspans[p]
        for js in ((0, 1), (2, 3)):
            for j, v in zip(js, partial(g, p, js, True)):
                psend[j, g, :, a:a + w] = v.astype(BF16)
                rcopy(j, g, p).start()

    def summed(g, p, js):
        a, w = rspans[p]
        for j, v in zip(js, partial(g, p, js, False)):
            rcopy(j, g, p).wait_recv()
            yield v + precv[j, g, :, a:a + w].astype(F32)

    def near(g, p):
        a, w = rspans[p]
        for j, v in enumerate(summed(g, p, (0, 1))):
            rsend[j, g, :, a:a + w] = v.astype(BF16)
            rcopy(4 + j, g, p).start()

    def home(g, p):
        a, w = rspans[p]
        far, v = summed(g, p, (2, 3))
        fin[1 - at.h, g, :, a:a + w] = far.astype(BF16)
        for k in range(2):
            rcopy(4 + k, g, p).wait_recv()
            v += rrecv[k, g, :, a:a + w].astype(F32)
        fin[at.h, g, :, a:a + w] = v.astype(BF16)
        back.start(*rpiece(g, p))
        for h in range(2):
            ret[h, g, mine, a:a + w] = fin[h, g, mine, a:a + w]

    def tcopy(p):
        a, w = rspans[p]
        return pltpu.make_async_remote_copy(
            src_ref=tsend.at[:, :, pl.ds(a, w)], dst_ref=trecv.at[:, :, pl.ds(a, w)],
            send_sem=t_sem.at[0, p], recv_sem=t_sem.at[1, p],
            device_id=at.to(2), device_id_type=MESH)

    def combine(_, p):
        a, w = rspans[p]
        if p == 0:
            for g in range(2):
                comb = selg[g].T
                hi = comb.astype(BF16)
                comb_hi[g] = hi
                comb_lo[g] = (comb - hi.astype(F32)).astype(BF16)
        for g in range(2):
            back.wait(*rpiece(g, p))
        total = jnp.zeros((toks, 2 * w), F32)
        for g in range(2):
            got = wide([ret[h, g, :, a:a + w] for h in range(2)])
            total += dot(comb_hi[g], got) + dot(comb_lo[g], got)
        for h in range(2):
            tsend[h, :, a:a + w] = total[:, h * w:(h + 1) * w].astype(BF16)
        tcopy(p).start()

    def weigh(_, p):
        a, w = rspans[p]
        tcopy(p).wait_recv()
        tangents = []
        for h in range(2):
            total = tsend[h, :, a:a + w].astype(F32) + trecv[h, :, a:a + w].astype(F32)
            tangents.append(total.astype(BF16))
        for g in range(2):
            rows = (dot(sel[g], wide(tangents)) * gsl[g]).astype(BF16)
            for h in range(2):
                wsend[h, g, :, a:a + w] = rows[:, h * w:(h + 1) * w]
        out_w.start(*wpiece(p))
        tan_ref[:, a:a + w] = jnp.where(at.h == 0, tangents[0], tangents[1])
        for h in range(2):
            for g in range(2):
                wbuf[at.c, at.b, h, g, mine, a:a + w] = wsend[h, g, mine, a:a + w]

    def w_one(_, p):
        out_w.wait(*wpiece(p))
        out_v.one(*wpiece(p))

    def w_two(_, p):
        out_v.two(*wpiece(p))

    def product(_, p):
        a, w = rspans[p]
        out_v.done(*wpiece(p))
        for k in range(0, 8, 2):
            c, b, h = cbh(k)
            v = sum(dot(hid_t[g], wide([wbuf[c, b, h, g, :, a:a + w] for c in range(2)]))
                    for g in range(2))
            for c in range(2):
                gn_ref[0, :, (k + c) * chunk + a:(k + c) * chunk + a + w] = v[:, c * w:(c + 1) * w]

    loads[0].wait()
    loads[1].wait()
    pl.semaphore_wait(barrier, experts - 1 + 4)
    steps = {
        "a": choose, "1": d_one, "2": d_two, "u": up, "s": silu, "t": to_pair, "n": near,
        "h": home, "c": combine, "w": weigh, "3": w_one, "4": w_two, "p": product}
    for kind, g, p in plan(dwidths, rwidths)[0]:
        if upto is None or kind in upto:
            steps[kind](g, p)

    for g in range(2):
        for p in range(nd):
            out_a.drain(*dpiece(g, p))
            out_g.drain(*dpiece(g, p))
    if upto is None:
        for p in range(nr):
            for g in range(2):
                back.drain(*rpiece(g, p))
                for kind in range(6):
                    rcopy(kind, g, p).wait_send()
            tcopy(p).wait_send()
            out_w.drain(*wpiece(p))
            out_v.drain(*wpiece(p))


def on_device(dwidths, rwidths, cap, upto, tokens, w_gate, w_up, tangent_down, gates, expert_ids):
    experts = lax.axis_size("ep")
    toks, width = tokens.shape
    chunk = width // 8
    hidden = w_gate.shape[2]
    half = experts * cap
    nd, nr = len(dwidths), len(rwidths)
    vmem, anywhere = pl.BlockSpec(memory_space=pltpu.VMEM), pl.BlockSpec(memory_space=pl.ANY)
    return pl.pallas_call(
        functools.partial(kernel, dwidths, rwidths, experts, cap, upto),
        out_shape=(
            pltpu.VMEM((1, hidden, width), F32),
            pltpu.VMEM((toks, chunk), BF16),
        ),
        in_specs=[vmem, vmem, anywhere, anywhere, anywhere, anywhere],
        out_specs=(vmem, vmem),
        scratch_shapes=[
            pltpu.VMEM((2, toks, chunk), BF16),
            pltpu.VMEM((width, hidden), BF16),
            pltpu.VMEM((width, hidden), BF16),
            pltpu.VMEM((8, hidden, chunk), BF16),
            pltpu.VMEM((2, half, toks), BF16),
            pltpu.VMEM((2, half, toks), F32),
            pltpu.VMEM((2, half, 1), F32),
            pltpu.VMEM((2, toks, half), BF16),
            pltpu.VMEM((2, toks, half), BF16),
            pltpu.VMEM((2, 2, half, chunk), BF16),
            pltpu.VMEM((2, 2, 2, 2, half, chunk), BF16),
            pltpu.VMEM((2, half, hidden), F32),
            pltpu.VMEM((2, half, hidden), F32),
            pltpu.VMEM((2, half, hidden), BF16),
            pltpu.VMEM((2, hidden, half), BF16),
            pltpu.VMEM((4, 2, half, chunk), BF16),
            pltpu.VMEM((4, 2, half, chunk), BF16),
            pltpu.VMEM((2, 2, half, chunk), BF16),
            pltpu.VMEM((2, 2, half, chunk), BF16),
            pltpu.VMEM((2, 2, half, chunk), BF16),
            pltpu.VMEM((2, 2, half, chunk), BF16),
            pltpu.VMEM((2, toks, chunk), BF16),
            pltpu.VMEM((2, toks, chunk), BF16),
            pltpu.VMEM((2, 2, half, chunk), BF16),
            pltpu.VMEM((2, 2, 2, 2, half, chunk), BF16),
            pltpu.SemaphoreType.DMA((12,)),
            pltpu.SemaphoreType.DMA((2, 2 * nd)),
            pltpu.SemaphoreType.DMA((2, 2 * nr)),
            pltpu.SemaphoreType.DMA((2, nr)),
            pltpu.SemaphoreType.DMA((2 * nd, 5)),
            pltpu.SemaphoreType.DMA((2 * nd, 5)),
            pltpu.SemaphoreType.DMA((nr, 5)),
            pltpu.SemaphoreType.DMA((nr, 5)),
            pltpu.SemaphoreType.DMA((2 * nr, 6)),
            pltpu.SemaphoreType.DMA((2 * nr, 6)),
            pltpu.SemaphoreType.DMA((2, nr)),
        ],
        compiler_params=pltpu.CompilerParams(
            collective_id=0, has_side_effects=True, vmem_limit_bytes=50 * 2**20),
    )(expert_ids.T, gates.T, tokens, w_gate, w_up, tangent_down)


def solution(mesh, dwidths=(128, 256, 256, 256), rwidths=(128,) * 7, cap=16, upto=None):
    in_specs = (
        P("ep", None),
        P("ep", None, "fsdp"),
        P("ep", None, "fsdp"),
        P("ep", "fsdp", None),
        P("ep", None),
        P("ep", None),
    )
    out_specs = (P("ep", "fsdp", None), P("ep", "fsdp"))
    return jax.shard_map(
        functools.partial(on_device, dwidths, rwidths, cap, upto),
        mesh=mesh, in_specs=in_specs, out_specs=out_specs, check_vma=False,
    )
```

```python
import functools

import jax
import jax.numpy as jnp
from jax import lax
from jax.experimental import pallas as pl
from jax.experimental.pallas import tpu as pltpu
from jax.sharding import PartitionSpec as P

MESH = pl.DeviceIdType.MESH
F32 = jnp.float32
BF16 = jnp.bfloat16


def spans(widths):
    out, at = [], 0
    for w in widths:
        out.append((at, w))
        at += w
    return out


def dot(a, b):
    return jnp.dot(a, b, preferred_element_type=F32)


def wide(blocks):
    return jnp.concatenate(blocks, axis=1)


def cbh(k):
    return k % 2, k // 2 % 2, k // 4


class Place:
    def __init__(self):
        self.e = lax.axis_index("ep")
        self.f = lax.axis_index("fsdp")
        self.x = self.f // 2
        self.c = self.f - 2 * self.x
        self.h = self.x // 2
        self.b = self.x - 2 * self.h

    def chip(self, off):
        return lax.rem(self.x + off, 4)

    def chunk(self, off, other=False):
        return 2 * self.chip(off) + (1 - self.c if other else self.c)

    def to(self, off):
        return (self.e, self.chunk(off))

    def pair(self):
        return (self.e, self.chunk(0, True))


class AllToAll:
    def __init__(self, at, experts, cap, src, dst, sems):
        self.__dict__.update(locals())

    def start(self, i, lead, a, w):
        at, cap = self.at, self.cap

        def one(d, carry):
            to = lax.rem(at.e + d, self.experts)
            there = pl.ds(pl.multiple_of(to * cap, cap), cap)
            here = pl.ds(pl.multiple_of(at.e * cap, cap), cap)
            pltpu.make_async_remote_copy(
                src_ref=self.src.at[(*lead, there, pl.ds(a, w))],
                dst_ref=self.dst.at[(*lead, here, pl.ds(a, w))],
                send_sem=self.sems.at[0, i],
                recv_sem=self.sems.at[1, i],
                device_id=(to, at.f),
                device_id_type=MESH,
            ).start()
            return carry

        lax.fori_loop(1, self.experts, one, 0)

    def _all(self, way, i, lead, a, w):
        ref = self.src.at[(*lead, pl.ds(0, (self.experts - 1) * self.cap), pl.ds(a, w))]
        pltpu.make_async_copy(ref, ref, self.sems.at[way, i]).wait()

    def wait(self, *piece):
        self._all(1, *piece)

    def drain(self, *piece):
        self._all(0, *piece)


class Gather:
    def __init__(self, at, buf, send, recv):
        self.__dict__.update(locals())

    def copy(self, kind, i, groups, a, w):
        at = self.at
        ref = self.buf.at[at.b, at.h, groups, :, pl.ds(a, w)]
        return pltpu.make_async_remote_copy(
            src_ref=ref,
            dst_ref=ref,
            send_sem=self.send.at[i, kind],
            recv_sem=self.recv.at[i, kind],
            device_id=at.to(1 if kind == 0 else 3),
            device_id_type=MESH,
        )

    def start(self, *piece):
        for kind in range(2):
            self.copy(kind, *piece).start()

    def wait(self, *piece):
        for kind in range(2):
            self.copy(kind, *piece).wait_recv()

    def drain(self, *piece):
        for kind in range(2):
            self.copy(kind, *piece).wait_send()


def plan(dwidths, rwidths, direct, delay=(3.0, 4.0, 2.5)):
    nd, nr = len(dwidths), len(rwidths)
    wd, wr = [w / 896 for w in dwidths], [w / 896 for w in rwidths]
    delay = dict(zip(("x", "yz", "pair"), delay))
    steps = {}
    for g in range(2):
        for p in range(nd):
            w, i = wd[p], g * nd + p
            if (g, p) in direct:
                steps["a", g, p] = (i, 0.4 + 2.4 * w, [], [("yz", 20 * w)])
                steps["u", g, p] = (90 + i, 2.4 * w, [("a", g, p), "weights"], [])
            else:
                steps["a", g, p] = (i, 0.4 + 1.2 * w, [], [("yz", 10 * w)])
                steps["1", g, p] = (i, 0.1, [("a", g, p)], [("x", 10 * w)])
                steps["u", g, p] = (90 + i, 2.4 * w, [("1", g, p), "weights"], [])
        steps["e", g, 0] = (99, 0.1, [("u", g, p) for p in range(nd)], [("pair", 2.0)])
        steps["s", g, 0] = (100, 1.0, [("e", g, 0)], [])
        for p in range(nr):
            w, i = wr[p], 20 + g * nr + p
            steps["n", g, p] = (i, 1.2 * w, [("s", g, 0)], [("x", 10 * w)])
            steps["h", g, p] = (i, 0.4 + 1.4 * w, [("n", g, p)], [("yz", 10 * w)])
    for p in range(nr):
        w, i = wr[p], 40 + p
        steps["c", 0, p] = (i, 1.4 * w, [("h", 0, p), ("h", 1, p)], [("x", 10 * w)])
        steps["w", 0, p] = (i, 0.4 + 1.6 * w, [("c", 0, p)], [("yz", 20 * w)])
        steps["3", 0, p] = (i, 0.1, [("w", 0, p)], [("x", 20 * w), ("pair", 4 * w)])
        steps["4", 0, p] = (i, 0.1, [("3", 0, p)], [("pair", 4 * w)])
        steps["p", 0, p] = (200 + i, 2.4 * w, [("4", 0, p)], [])
    now, free, order = 0.0, {"x": 0.0, "yz": 0.0, "pair": 0.0}, []
    there = {"weights": 11.0}
    while len(order) < len(steps):
        left = [s for s in steps if s not in there and all(q in there for q in steps[s][2])]
        at = {s: max([there[q] for q in steps[s][2]], default=0.0) for s in left}
        ready = [s for s in left if at[s] <= now]
        if not ready:
            now = min(at.values())
            continue
        step = min(ready, key=lambda s: (steps[s][0], s))
        now += steps[step][1]
        there[step] = now
        for link, time in steps[step][3]:
            free[link] = max(free[link], now) + time
            there[step] = max(there[step], free[link] + delay[link])
        order.append(step)
    return order, now


def kernel(
    dwidths, rwidths, direct, experts, cap, options,
    ids_hbm, gates_hbm, tok_ref, wg_ref, wu_ref, td_ref,
    gn_ref, tan_ref,
    ids_ref, gates_ref, tokv, wgv, wuv, tdv, sel, selg, gsl, comb_hi, comb_lo, send, xbuf, acc,
    acc_in, hid, hid_t, rsend, rrecv, fin, ret, tsend, trecv, wsend, wbuf,
    load, v_sem, x_sem, h_sem, w_sem, xg_send, xg_recv, g_send, g_recv, p_sem, e_sem, r_send,
    r_recv, t_sem,
):
    at = Place()
    dspans, rspans = spans(dwidths), spans(rwidths)
    nd, nr = len(dspans), len(rspans)
    toks, chunk = tokv.shape[2:]
    hidden = gn_ref.shape[1]
    half = experts * cap
    ranks = 2 * cap
    both = slice(None)
    chips = [(b, h) for h in range(2) for b in range(2)]

    barrier = pltpu.get_barrier_semaphore()

    def greet(d, carry):
        pl.semaphore_signal(
            barrier, inc=1, device_id=(lax.rem(at.e + d, experts), at.f), device_id_type=MESH)
        return carry

    lax.fori_loop(1, experts, greet, 0)
    for to in (at.to(1), at.to(3), at.to(2), at.pair()):
        pl.semaphore_signal(barrier, inc=1, device_id=to, device_id_type=MESH)

    def columns(x, c):
        return pl.ds(pl.multiple_of((2 * x + c) * chunk, 128), chunk)

    own = pl.ds(pl.multiple_of(at.c * hidden, 128), hidden)

    def weights(x, c):
        return [(wg_ref.at[0, columns(x, c), :], wgv.at[x, :, own]),
                (wu_ref.at[0, columns(x, c), :], wuv.at[x, :, own]),
                (td_ref.at[0, :, columns(x, c)], tdv.at[x, own, :])]

    loads = [pltpu.make_async_copy(ids_hbm, ids_ref, load.at[0]),
             pltpu.make_async_copy(gates_hbm, gates_ref, load.at[1])]
    loads += [pltpu.make_async_copy(
        tok_ref.at[:, columns(2 * h + b, at.c)], tokv.at[b, h], load.at[2 + 2 * h + b])
        for b, h in chips]
    local, shared = [], []
    for x in range(4):
        for k, (src, dst) in enumerate(weights(x, at.c)):
            local.append(pltpu.make_async_copy(src, dst, load.at[6 + 3 * x + k]))
        for k, (src, dst) in enumerate(weights(x, 1 - at.c)):
            shared.append(pltpu.make_async_remote_copy(
                src_ref=src, dst_ref=dst, send_sem=v_sem.at[0, 3 * x + k],
                recv_sem=v_sem.at[1, 3 * x + k], device_id=at.pair(), device_id_type=MESH))
    for copy in loads + local:
        copy.start()
    loads[0].wait()
    loads[1].wait()

    expert = lax.broadcasted_iota(jnp.int32, (experts, toks), 0)
    named = [ids_ref[k:k + 1, :] == expert for k in range(ids_ref.shape[0])]
    mask_t = sum(jnp.where(m, 1.0, 0.0) for m in named)
    gate_t = sum(jnp.where(m, gates_ref[k:k + 1, :], 0.0) for k, m in enumerate(named))
    earlier = jnp.where(
        lax.broadcasted_iota(jnp.int32, (toks, toks), 0)
        < lax.broadcasted_iota(jnp.int32, (toks, toks), 1), 1.0, 0.0)
    rank_t = dot(mask_t.astype(BF16), earlier.astype(BF16))
    place = lax.broadcasted_iota(jnp.int32, (ranks, toks), 0).astype(F32)
    for k in range(experts):
        here = (rank_t[k:k + 1, :] == place) & (mask_t[k:k + 1, :] > 0.5)
        picked = jnp.where(here, gate_t[k:k + 1, :], 0.0)
        one = jnp.where(here, 1.0, 0.0).astype(BF16)
        total = jnp.sum(picked, axis=1, keepdims=True)
        for g in range(2):
            r, part = slice(k * cap, (k + 1) * cap), slice(g * cap, (g + 1) * cap)
            sel[g, r, :] = one[part]
            selg[g, r, :] = picked[part]
            gsl[g, r, :] = total[part]

    mine = pl.ds(pl.multiple_of(at.e * cap, cap), cap)
    out_a = AllToAll(at, experts, cap, send, xbuf, x_sem)
    out_g = Gather(at, xbuf, xg_send, xg_recv)
    back = AllToAll(at, experts, cap, fin, ret, h_sem)
    out_w = AllToAll(at, experts, cap, wsend, wbuf.at[at.c], w_sem)
    out_v = Gather(at, wbuf.at[at.c], g_send, g_recv)

    def apiece(g, p):
        lead = (both, both, g) if (g, p) in direct else (at.b, both, g)
        return g * nd + p, lead, *dspans[p]

    def xpiece(g, p):
        return g * nd + p, g, *dspans[p]

    def hpiece(g, p):
        return g * nr + p, (both, g), *rspans[p]

    def wpiece(p):
        return p, (at.b, both, both), *rspans[p]

    def vpiece(p):
        return p, both, *rspans[p]

    def choose(g, p):
        a, w = dspans[p]
        if (g, p) in direct:
            which = [(b, h) for b, h in chips]
        else:
            which = [(at.b, h) for h in range(2)]
        rows = dot(sel[g], wide([tokv[b, h, :, a:a + w] for b, h in which])).astype(BF16)
        for k, (b, h) in enumerate(which):
            send[b, h, g, :, a:a + w] = rows[:, k * w:(k + 1) * w]
        out_a.start(*apiece(g, p))
        for b, h in which:
            xbuf[b, h, g, mine, a:a + w] = send[b, h, g, mine, a:a + w]

    def d_one(g, p):
        out_a.wait(*apiece(g, p))
        out_g.start(*xpiece(g, p))

    def up(g, p):
        a, w = dspans[p]
        if (g, p) == first_up:
            for x in range(4):
                for k in range(2):
                    local[3 * x + k].wait()
                    shared[3 * x + k].wait_recv()
        if (g, p) in direct:
            out_a.wait(*apiece(g, p))
        else:
            out_g.wait(*xpiece(g, p))
        for n, matrix in enumerate((wgv, wuv)):
            cols = slice(n * 2 * hidden, (n + 1) * 2 * hidden)
            total = None if up_seen[g] == 0 else acc[g, :, cols]
            for h in range(2):
                part = dot(
                    wide([xbuf[b, h, g, :, a:a + w] for b in range(2)]),
                    jnp.concatenate([matrix[2 * h + b, a:a + w, :] for b in range(2)], axis=0))
                total = part if total is None else total + part
            acc[g, :, cols] = total
        up_seen[g] += 1

    def ecopy(g):
        return pltpu.make_async_remote_copy(
            src_ref=acc.at[g], dst_ref=acc_in.at[g], send_sem=e_sem.at[0, g],
            recv_sem=e_sem.at[1, g], device_id=at.pair(), device_id_type=MESH)

    def exchange(g, _):
        ecopy(g).start()

    def silu(g, _):
        ecopy(g).wait_recv()

        def tile(m, carry):
            r = pl.ds(pl.multiple_of(m * cap, cap), cap)
            v = acc[g, r, :] + acc_in[g, r, :]
            gate, value = v[:, :2 * hidden], v[:, 2 * hidden:]
            hid[g, r, :] = (gate / (1.0 + jnp.exp(-gate)) * value).astype(BF16)
            return carry

        lax.fori_loop(0, half // cap, tile, 0)
        if g == 0:
            for x in range(4):
                local[3 * x + 2].wait()
                shared[3 * x + 2].wait_recv()

    offs = (1, 3, 2, 0)

    def rcopy(kind, g, p):
        a, w = rspans[p]
        return pltpu.make_async_remote_copy(
            src_ref=rsend.at[kind, g, :, pl.ds(a, w)], dst_ref=rrecv.at[kind, g, :, pl.ds(a, w)],
            send_sem=r_send.at[g * nr + p, kind], recv_sem=r_recv.at[g * nr + p, kind],
            device_id=at.to(1 if kind == 0 else 3), device_id_type=MESH)

    def partial(g, p, js):
        a, w = rspans[p]
        v = dot(hid[g], wide([tdv[at.chip(offs[j]), :, a:a + w] for j in js]))
        return [v[:, i * w:(i + 1) * w] for i in range(len(js))]

    def near(g, p):
        a, w = rspans[p]
        for j, v in enumerate(partial(g, p, (0, 1))):
            rsend[j, g, :, a:a + w] = v.astype(BF16)
            rcopy(j, g, p).start()

    def home(g, p):
        a, w = rspans[p]
        far, v = partial(g, p, (2, 3))
        fin[1 - at.h, g, :, a:a + w] = far.astype(BF16)
        for k in range(2):
            rcopy(k, g, p).wait_recv()
            v += rrecv[k, g, :, a:a + w].astype(F32)
        fin[at.h, g, :, a:a + w] = v.astype(BF16)
        back.start(*hpiece(g, p))
        for h in range(2):
            ret[h, g, mine, a:a + w] = fin[h, g, mine, a:a + w]

    def tcopy(p):
        a, w = rspans[p]
        return pltpu.make_async_remote_copy(
            src_ref=tsend.at[:, :, pl.ds(a, w)], dst_ref=trecv.at[:, :, pl.ds(a, w)],
            send_sem=t_sem.at[0, p], recv_sem=t_sem.at[1, p],
            device_id=at.to(2), device_id_type=MESH)

    def combine(_, p):
        a, w = rspans[p]
        if p == 0:
            for g in range(2):
                comb = selg[g].T
                hi = comb.astype(BF16)
                comb_hi[g] = hi
                comb_lo[g] = (comb - hi.astype(F32)).astype(BF16)
        for g in range(2):
            back.wait(*hpiece(g, p))
        total = jnp.zeros((toks, 2 * w), F32)
        for g in range(2):
            got = wide([ret[h, g, :, a:a + w] for h in range(2)])
            total += dot(comb_hi[g], got) + dot(comb_lo[g], got)
        for h in range(2):
            tsend[h, :, a:a + w] = total[:, h * w:(h + 1) * w].astype(BF16)
        tcopy(p).start()

    def weigh(_, p):
        a, w = rspans[p]
        tcopy(p).wait_recv()
        tangents = []
        for h in range(2):
            total = tsend[h, :, a:a + w].astype(F32) + trecv[h, :, a:a + w].astype(F32)
            tangents.append(total.astype(BF16))
        for g in range(2):
            rows = (dot(sel[g], wide(tangents)) * gsl[g]).astype(BF16)
            for h in range(2):
                wsend[at.b, h, g, :, a:a + w] = rows[:, h * w:(h + 1) * w]
        out_w.start(*wpiece(p))
        tan_ref[:, a:a + w] = jnp.where(at.h == 0, tangents[0], tangents[1])
        for h in range(2):
            for g in range(2):
                wbuf[at.c, at.b, h, g, mine, a:a + w] = wsend[at.b, h, g, mine, a:a + w]

    def pcopy(kind, p):
        a, w = rspans[p]
        if kind == 0:
            ref = wbuf.at[at.c, at.b, :, :, :, pl.ds(a, w)]
        else:
            ref = wbuf.at[at.c, 1 - at.b, at.chip(3 if kind == 1 else 1) // 2, :, :, pl.ds(a, w)]
        return pltpu.make_async_remote_copy(
            src_ref=ref, dst_ref=ref, send_sem=p_sem.at[0, p, kind],
            recv_sem=p_sem.at[1, p, kind], device_id=at.pair(), device_id_type=MESH)

    def w_one(_, p):
        out_w.wait(*wpiece(p))
        out_v.start(*vpiece(p))
        pcopy(0, p).start()

    def w_two(_, p):
        for kind in range(2):
            out_v.copy(kind, *vpiece(p)).wait_recv()
            pcopy(1 + kind, p).start()

    def product(_, p):
        a, w = rspans[p]
        if p == 0:
            for g in range(2):
                hid_t[g] = hid[g, :, own].astype(F32).T.astype(BF16)
        for kind in range(3):
            pcopy(kind, p).wait_recv()
        for k in range(0, 8, 2):
            c, b, h = cbh(k)
            v = sum(dot(hid_t[g], wide([wbuf[c, b, h, g, :, a:a + w] for c in range(2)]))
                    for g in range(2))
            for c in range(2):
                gn_ref[0, :, (k + c) * chunk + a:(k + c) * chunk + a + w] = v[:, c * w:(c + 1) * w]

    for copy in loads[2:]:
        copy.wait()
    pl.semaphore_wait(barrier, experts - 1 + 4)
    steps = {
        "a": choose, "1": d_one, "u": up, "e": exchange, "s": silu, "n": near,
        "h": home, "c": combine, "w": weigh, "3": w_one, "4": w_two, "p": product}
    order = plan(dwidths, rwidths, direct, *options)[0]
    first_up = [step for step in order if step[0] == "u"][0][1:]
    up_seen = [0, 0]
    for count, (kind, g, p) in enumerate(order):
        steps[kind](g, p)
        if count == 0:
            for k in (0, 1, 2):
                for x in range(4):
                    shared[3 * x + k].start()

    for copy in shared:
        copy.wait_send()
    for g in range(2):
        ecopy(g).wait_send()
        for p in range(nd):
            out_a.drain(*apiece(g, p))
            if (g, p) not in direct:
                out_g.drain(*xpiece(g, p))
    for p in range(nr):
        for g in range(2):
            back.drain(*hpiece(g, p))
            for kind in range(2):
                rcopy(kind, g, p).wait_send()
        tcopy(p).wait_send()
        out_w.drain(*wpiece(p))
        out_v.drain(*vpiece(p))
        for kind in range(3):
            pcopy(kind, p).wait_send()


def on_device(
    dwidths, rwidths, direct, cap, options, tokens, w_gate, w_up, tangent_down, gates, expert_ids
):
    experts = lax.axis_size("ep")
    toks, width = tokens.shape
    topk = gates.shape[1]
    chunk = width // 8
    hidden = w_gate.shape[2]
    half = experts * cap
    nd, nr = len(dwidths), len(rwidths)
    vmem, anywhere = pl.BlockSpec(memory_space=pltpu.VMEM), pl.BlockSpec(memory_space=pl.ANY)
    return pl.pallas_call(
        functools.partial(kernel, dwidths, rwidths, direct, experts, cap, options),
        out_shape=(
            pltpu.VMEM((1, hidden, width), F32),
            pltpu.VMEM((toks, chunk), BF16),
        ),
        in_specs=[anywhere] * 6,
        out_specs=(vmem, vmem),
        scratch_shapes=[
            pltpu.VMEM((topk, toks), jnp.int32),
            pltpu.VMEM((topk, toks), F32),
            pltpu.VMEM((2, 2, toks, chunk), BF16),
            pltpu.VMEM((4, chunk, 2 * hidden), BF16),
            pltpu.VMEM((4, chunk, 2 * hidden), BF16),
            pltpu.VMEM((4, 2 * hidden, chunk), BF16),
            pltpu.VMEM((2, half, toks), BF16),
            pltpu.VMEM((2, half, toks), F32),
            pltpu.VMEM((2, half, 1), F32),
            pltpu.VMEM((2, toks, half), BF16),
            pltpu.VMEM((2, toks, half), BF16),
            pltpu.VMEM((2, 2, 2, half, chunk), BF16),
            pltpu.VMEM((2, 2, 2, half, chunk), BF16),
            pltpu.VMEM((2, half, 4 * hidden), F32),
            pltpu.VMEM((2, half, 4 * hidden), F32),
            pltpu.VMEM((2, half, 2 * hidden), BF16),
            pltpu.VMEM((2, hidden, half), BF16),
            pltpu.VMEM((2, 2, half, chunk), BF16),
            pltpu.VMEM((2, 2, half, chunk), BF16),
            pltpu.VMEM((2, 2, half, chunk), BF16),
            pltpu.VMEM((2, 2, half, chunk), BF16),
            pltpu.VMEM((2, toks, chunk), BF16),
            pltpu.VMEM((2, toks, chunk), BF16),
            pltpu.VMEM((2, 2, 2, half, chunk), BF16),
            pltpu.VMEM((2, 2, 2, 2, half, chunk), BF16),
            pltpu.SemaphoreType.DMA((18,)),
            pltpu.SemaphoreType.DMA((2, 12)),
            pltpu.SemaphoreType.DMA((2, 2 * nd)),
            pltpu.SemaphoreType.DMA((2, 2 * nr)),
            pltpu.SemaphoreType.DMA((2, nr)),
            pltpu.SemaphoreType.DMA((2 * nd, 2)),
            pltpu.SemaphoreType.DMA((2 * nd, 2)),
            pltpu.SemaphoreType.DMA((nr, 2)),
            pltpu.SemaphoreType.DMA((nr, 2)),
            pltpu.SemaphoreType.DMA((2, nr, 3)),
            pltpu.SemaphoreType.DMA((2, 2)),
            pltpu.SemaphoreType.DMA((2 * nr, 2)),
            pltpu.SemaphoreType.DMA((2 * nr, 2)),
            pltpu.SemaphoreType.DMA((2, nr)),
        ],
        compiler_params=pltpu.CompilerParams(
            collective_id=0, has_side_effects=True, vmem_limit_bytes=50 * 2**20),
    )(expert_ids.T, gates.T, tokens, w_gate, w_up, tangent_down)


def solution(
    mesh, dwidths=(128,) * 7, rwidths=(128,) * 7, direct=((1, 6),), cap=16, options=()
):
    in_specs = (
        P("ep", None),
        P("ep", None, "fsdp"),
        P("ep", None, "fsdp"),
        P("ep", "fsdp", None),
        P("ep", None),
        P("ep", None),
    )
    out_specs = (P("ep", "fsdp", None), P("ep", "fsdp"))
    return jax.shard_map(
        functools.partial(on_device, dwidths, rwidths, direct, cap, options),
        mesh=mesh, in_specs=in_specs, out_specs=out_specs, check_vma=False,
    )
```

```python
import functools

import jax
import jax.numpy as jnp
from jax import lax
from jax.experimental import pallas as pl
from jax.experimental.pallas import tpu as pltpu
from jax.sharding import PartitionSpec as P

MESH = pl.DeviceIdType.MESH
F32 = jnp.float32
BF16 = jnp.bfloat16


def spans(widths):
    out, at = [], 0
    for w in widths:
        out.append((at, w))
        at += w
    return out


def dot(a, b):
    return jnp.dot(a, b, preferred_element_type=F32)


def wide(blocks):
    return jnp.concatenate(blocks, axis=1)


def cbh(k):
    return k % 2, k // 2 % 2, k // 4


class Place:
    def __init__(self):
        self.e = lax.axis_index("ep")
        self.f = lax.axis_index("fsdp")
        self.x = self.f // 2
        self.c = self.f - 2 * self.x
        self.h = self.x // 2
        self.b = self.x - 2 * self.h

    def chip(self, off):
        return lax.rem(self.x + off, 4)

    def chunk(self, off, other=False):
        return 2 * self.chip(off) + (1 - self.c if other else self.c)

    def to(self, off):
        return (self.e, self.chunk(off))

    def pair(self):
        return (self.e, self.chunk(0, True))


class AllToAll:
    def __init__(self, at, experts, cap, src, dst, sems):
        self.__dict__.update(locals())

    def start(self, i, lead, a, w):
        at, cap = self.at, self.cap

        def one(d, carry):
            to = lax.rem(at.e + d, self.experts)
            there = pl.ds(pl.multiple_of(to * cap, cap), cap)
            here = pl.ds(pl.multiple_of(at.e * cap, cap), cap)
            pltpu.make_async_remote_copy(
                src_ref=self.src.at[(*lead, there, pl.ds(a, w))],
                dst_ref=self.dst.at[(*lead, here, pl.ds(a, w))],
                send_sem=self.sems.at[0, i],
                recv_sem=self.sems.at[1, i],
                device_id=(to, at.f),
                device_id_type=MESH,
            ).start()
            return carry

        lax.fori_loop(1, self.experts, one, 0)

    def _all(self, way, i, lead, a, w):
        ref = self.src.at[(*lead, pl.ds(0, (self.experts - 1) * self.cap), pl.ds(a, w))]
        pltpu.make_async_copy(ref, ref, self.sems.at[way, i]).wait()

    def wait(self, *piece):
        self._all(1, *piece)

    def drain(self, *piece):
        self._all(0, *piece)


class Gather:
    def __init__(self, at, buf, send, recv):
        self.__dict__.update(locals())

    def copy(self, kind, i, groups, a, w):
        at = self.at
        ref = self.buf.at[at.b, at.h, groups, :, pl.ds(a, w)]
        return pltpu.make_async_remote_copy(
            src_ref=ref,
            dst_ref=ref,
            send_sem=self.send.at[i, kind],
            recv_sem=self.recv.at[i, kind],
            device_id=at.to(1 if kind == 0 else 3),
            device_id_type=MESH,
        )

    def start(self, *piece):
        for kind in range(2):
            self.copy(kind, *piece).start()

    def wait(self, *piece):
        for kind in range(2):
            self.copy(kind, *piece).wait_recv()

    def drain(self, *piece):
        for kind in range(2):
            self.copy(kind, *piece).wait_send()


def plan(dwidths, rwidths, direct, wdirect, delay=(3.0, 4.0, 2.5)):
    nd, nr = len(dwidths), len(rwidths)
    wd, wr = [w / 896 for w in dwidths], [w / 896 for w in rwidths]
    delay = dict(zip(("x", "yz", "pair"), delay))
    steps = {}
    for g in range(2):
        for p in range(nd):
            w, i = wd[p], g * nd + p
            if (g, p) in direct:
                steps["a", g, p] = (i, 0.4 + 2.4 * w, [], [("yz", 20 * w)])
                steps["u", g, p] = (90 + i, 2.4 * w, [("a", g, p), "weights"], [])
            else:
                steps["a", g, p] = (i, 0.4 + 1.2 * w, [], [("yz", 10 * w)])
                steps["1", g, p] = (i, 0.1, [("a", g, p)], [("x", 10 * w)])
                steps["u", g, p] = (90 + i, 2.4 * w, [("1", g, p), "weights"], [])
        steps["e", g, 0] = (99, 0.1, [("u", g, p) for p in range(nd)], [("pair", 2.0)])
        steps["s", g, 0] = (100, 1.0, [("e", g, 0)], [])
        for p in range(nr):
            w, i = wr[p], 20 + g * nr + p
            steps["n", g, p] = (i, 1.2 * w, [("s", g, 0)], [("x", 10 * w)])
            steps["h", g, p] = (i, 0.4 + 1.4 * w, [("n", g, p)], [("yz", 10 * w)])
    for p in range(nr):
        w, i = wr[p], 40 + p
        steps["c", 0, p] = (i, 1.4 * w, [("h", 0, p), ("h", 1, p)], [("x", 10 * w)])
        if p in wdirect:
            steps["w", 0, p] = (i, 0.4 + 1.6 * w, [("c", 0, p)], [("x", 5 * w), ("yz", 20 * w)])
            steps["v", 0, p] = (i, 0.4 + 1.6 * w, [("x", 0, p)], [("yz", 20 * w)])
            steps["3", 0, p] = (i, 0.1, [("w", 0, p)], [("pair", 4 * w)])
            steps["4", 0, p] = (i, 0.1, [("3", 0, p), ("v", 0, p)], [("pair", 4 * w)])
        else:
            steps["w", 0, p] = (i, 0.4 + 1.6 * w, [("c", 0, p)], [("yz", 20 * w)])
            steps["3", 0, p] = (i, 0.1, [("w", 0, p)], [("x", 20 * w), ("pair", 4 * w)])
            steps["4", 0, p] = (i, 0.1, [("3", 0, p)], [("pair", 4 * w)])
        steps["p", 0, p] = (200 + i, 2.4 * w, [("4", 0, p)], [])
    now, free, order = 0.0, {"x": 0.0, "yz": 0.0, "pair": 0.0}, []
    there = {"weights": 11.0}
    while len(order) < len(steps):
        left = [s for s in steps if s not in there and all(q in there for q in steps[s][2])]
        at = {s: max([there[q] for q in steps[s][2]], default=0.0) for s in left}
        ready = [s for s in left if at[s] <= now]
        if not ready:
            now = min(at.values())
            continue
        step = min(ready, key=lambda s: (steps[s][0], s))
        now += steps[step][1]
        there[step] = now
        for link, time in steps[step][3]:
            free[link] = max(free[link], now) + time
            there[step] = max(there[step], free[link] + delay[link])
            if step[0] == "w" and link == "x":
                there["x", 0, step[2]] = there[step]
        order.append(step)
    return order, now


def kernel(
    dwidths, rwidths, direct, wdirect, experts, cap, options,
    ids_hbm, gates_hbm, tok_ref, wg_ref, wu_ref, td_ref,
    gn_ref, tan_ref,
    ids_ref, gates_ref, tokv, wgv, wuv, tdv, sel, selg, gsl, comb_hi, comb_lo, send, xbuf, acc,
    acc_in, hid, hid_t, rsend, rrecv, fin, ret, tsend, trecv, tang, wsend, wbuf,
    load, v_sem, x_sem, h_sem, w_sem, xg_send, xg_recv, g_send, g_recv, p_sem, e_sem, r_send,
    r_recv, t_sem, u_sem, w2_sem,
):
    at = Place()
    dspans, rspans = spans(dwidths), spans(rwidths)
    nd, nr = len(dspans), len(rspans)
    toks, chunk = tokv.shape[2:]
    hidden = gn_ref.shape[1]
    half = experts * cap
    ranks = 2 * cap
    both = slice(None)
    chips = [(b, h) for h in range(2) for b in range(2)]

    barrier = pltpu.get_barrier_semaphore()

    def greet(d, carry):
        pl.semaphore_signal(
            barrier, inc=1, device_id=(lax.rem(at.e + d, experts), at.f), device_id_type=MESH)
        return carry

    lax.fori_loop(1, experts, greet, 0)
    for to in (at.to(1), at.to(3), at.to(2), at.pair()):
        pl.semaphore_signal(barrier, inc=1, device_id=to, device_id_type=MESH)

    def columns(x, c):
        return pl.ds(pl.multiple_of((2 * x + c) * chunk, 128), chunk)

    own = pl.ds(pl.multiple_of(at.c * hidden, 128), hidden)

    def weights(x, c):
        return [(wg_ref.at[0, columns(x, c), :], wgv.at[x, :, own]),
                (wu_ref.at[0, columns(x, c), :], wuv.at[x, :, own]),
                (td_ref.at[0, :, columns(x, c)], tdv.at[x, own, :])]

    loads = [pltpu.make_async_copy(ids_hbm, ids_ref, load.at[0]),
             pltpu.make_async_copy(gates_hbm, gates_ref, load.at[1])]
    loads += [pltpu.make_async_copy(
        tok_ref.at[:, columns(2 * h + b, at.c)], tokv.at[b, h], load.at[2 + 2 * h + b])
        for b, h in chips]
    local, shared = [], []
    for x in range(4):
        for k, (src, dst) in enumerate(weights(x, at.c)):
            local.append(pltpu.make_async_copy(src, dst, load.at[6 + 3 * x + k]))
        for k, (src, dst) in enumerate(weights(x, 1 - at.c)):
            shared.append(pltpu.make_async_remote_copy(
                src_ref=src, dst_ref=dst, send_sem=v_sem.at[0, 3 * x + k],
                recv_sem=v_sem.at[1, 3 * x + k], device_id=at.pair(), device_id_type=MESH))
    for copy in loads + local:
        copy.start()
    loads[0].wait()
    loads[1].wait()

    expert = lax.broadcasted_iota(jnp.int32, (experts, toks), 0)
    named = [ids_ref[k:k + 1, :] == expert for k in range(ids_ref.shape[0])]
    mask_t = sum(jnp.where(m, 1.0, 0.0) for m in named)
    gate_t = sum(jnp.where(m, gates_ref[k:k + 1, :], 0.0) for k, m in enumerate(named))
    earlier = jnp.where(
        lax.broadcasted_iota(jnp.int32, (toks, toks), 0)
        < lax.broadcasted_iota(jnp.int32, (toks, toks), 1), 1.0, 0.0)
    rank_t = dot(mask_t.astype(BF16), earlier.astype(BF16))
    place = lax.broadcasted_iota(jnp.int32, (ranks, toks), 0).astype(F32)
    for k in range(experts):
        here = (rank_t[k:k + 1, :] == place) & (mask_t[k:k + 1, :] > 0.5)
        picked = jnp.where(here, gate_t[k:k + 1, :], 0.0)
        one = jnp.where(here, 1.0, 0.0).astype(BF16)
        total = jnp.sum(picked, axis=1, keepdims=True)
        for g in range(2):
            r, part = slice(k * cap, (k + 1) * cap), slice(g * cap, (g + 1) * cap)
            sel[g, r, :] = one[part]
            selg[g, r, :] = picked[part]
            gsl[g, r, :] = total[part]

    mine = pl.ds(pl.multiple_of(at.e * cap, cap), cap)
    out_a = AllToAll(at, experts, cap, send, xbuf, x_sem)
    out_g = Gather(at, xbuf, xg_send, xg_recv)
    back = AllToAll(at, experts, cap, fin, ret, h_sem)
    out_w = AllToAll(at, experts, cap, wsend, wbuf.at[at.c], w_sem)
    out_w2 = AllToAll(at, experts, cap, wsend, wbuf.at[at.c], w2_sem)
    out_v = Gather(at, wbuf.at[at.c], g_send, g_recv)

    def apiece(g, p):
        lead = (both, both, g) if (g, p) in direct else (at.b, both, g)
        return g * nd + p, lead, *dspans[p]

    def xpiece(g, p):
        return g * nd + p, g, *dspans[p]

    def hpiece(g, p):
        return g * nr + p, (both, g), *rspans[p]

    def wpiece(p):
        return p, (at.b, both, both), *rspans[p]

    def w2piece(p):
        return p, (1 - at.b, both, both), *rspans[p]

    def vpiece(p):
        return p, both, *rspans[p]

    def choose(g, p):
        a, w = dspans[p]
        if (g, p) in direct:
            which = [(b, h) for b, h in chips]
        else:
            which = [(at.b, h) for h in range(2)]
        rows = dot(sel[g], wide([tokv[b, h, :, a:a + w] for b, h in which])).astype(BF16)
        for k, (b, h) in enumerate(which):
            send[b, h, g, :, a:a + w] = rows[:, k * w:(k + 1) * w]
        out_a.start(*apiece(g, p))
        for b, h in which:
            xbuf[b, h, g, mine, a:a + w] = send[b, h, g, mine, a:a + w]

    def d_one(g, p):
        out_a.wait(*apiece(g, p))
        out_g.start(*xpiece(g, p))

    def up(g, p):
        a, w = dspans[p]
        if (g, p) == first_up:
            for x in range(4):
                for k in range(2):
                    local[3 * x + k].wait()
                    shared[3 * x + k].wait_recv()
        if (g, p) in direct:
            out_a.wait(*apiece(g, p))
        else:
            out_g.wait(*xpiece(g, p))
        for n, matrix in enumerate((wgv, wuv)):
            cols = slice(n * 2 * hidden, (n + 1) * 2 * hidden)
            total = None if up_seen[g] == 0 else acc[g, :, cols]
            for h in range(2):
                part = dot(
                    wide([xbuf[b, h, g, :, a:a + w] for b in range(2)]),
                    jnp.concatenate([matrix[2 * h + b, a:a + w, :] for b in range(2)], axis=0))
                total = part if total is None else total + part
            acc[g, :, cols] = total
        up_seen[g] += 1

    def ecopy(g):
        return pltpu.make_async_remote_copy(
            src_ref=acc.at[g], dst_ref=acc_in.at[g], send_sem=e_sem.at[0, g],
            recv_sem=e_sem.at[1, g], device_id=at.pair(), device_id_type=MESH)

    def exchange(g, _):
        ecopy(g).start()

    def silu(g, _):
        ecopy(g).wait_recv()

        def tile(m, carry):
            r = pl.ds(pl.multiple_of(m * cap, cap), cap)
            v = acc[g, r, :] + acc_in[g, r, :]
            gate, value = v[:, :2 * hidden], v[:, 2 * hidden:]
            hid[g, r, :] = (gate / (1.0 + jnp.exp(-gate)) * value).astype(BF16)
            return carry

        lax.fori_loop(0, half // cap, tile, 0)
        if g == 0:
            for x in range(4):
                local[3 * x + 2].wait()
                shared[3 * x + 2].wait_recv()

    offs = (1, 3, 2, 0)

    def rcopy(kind, g, p):
        a, w = rspans[p]
        return pltpu.make_async_remote_copy(
            src_ref=rsend.at[kind, g, :, pl.ds(a, w)], dst_ref=rrecv.at[kind, g, :, pl.ds(a, w)],
            send_sem=r_send.at[g * nr + p, kind], recv_sem=r_recv.at[g * nr + p, kind],
            device_id=at.to(1 if kind == 0 else 3), device_id_type=MESH)

    def partial(g, p, js):
        a, w = rspans[p]
        v = dot(hid[g], wide([tdv[at.chip(offs[j]), :, a:a + w] for j in js]))
        return [v[:, i * w:(i + 1) * w] for i in range(len(js))]

    def near(g, p):
        a, w = rspans[p]
        for j, v in enumerate(partial(g, p, (0, 1))):
            rsend[j, g, :, a:a + w] = v.astype(BF16)
            rcopy(j, g, p).start()

    def home(g, p):
        a, w = rspans[p]
        far, v = partial(g, p, (2, 3))
        fin[1 - at.h, g, :, a:a + w] = far.astype(BF16)
        for k in range(2):
            rcopy(k, g, p).wait_recv()
            v += rrecv[k, g, :, a:a + w].astype(F32)
        fin[at.h, g, :, a:a + w] = v.astype(BF16)
        back.start(*hpiece(g, p))
        for h in range(2):
            ret[h, g, mine, a:a + w] = fin[h, g, mine, a:a + w]

    def tcopy(p):
        a, w = rspans[p]
        return pltpu.make_async_remote_copy(
            src_ref=tsend.at[:, :, pl.ds(a, w)], dst_ref=trecv.at[:, :, pl.ds(a, w)],
            send_sem=t_sem.at[0, p], recv_sem=t_sem.at[1, p],
            device_id=at.to(2), device_id_type=MESH)

    def combine(_, p):
        a, w = rspans[p]
        if p == 0:
            for g in range(2):
                comb = selg[g].T
                hi = comb.astype(BF16)
                comb_hi[g] = hi
                comb_lo[g] = (comb - hi.astype(F32)).astype(BF16)
        for g in range(2):
            back.wait(*hpiece(g, p))
        total = jnp.zeros((toks, 2 * w), F32)
        for g in range(2):
            got = wide([ret[h, g, :, a:a + w] for h in range(2)])
            total += dot(comb_hi[g], got) + dot(comb_lo[g], got)
        for h in range(2):
            tsend[h, :, a:a + w] = total[:, h * w:(h + 1) * w].astype(BF16)
        tcopy(p).start()

    def ucopy(kind, p):
        a, w = rspans[p]
        ref = tang.at[at.b, at.h, :, pl.ds(a, w)]
        return pltpu.make_async_remote_copy(
            src_ref=ref, dst_ref=ref, send_sem=u_sem.at[0, p, kind],
            recv_sem=u_sem.at[1, p, kind], device_id=at.to(1 if kind == 0 else 3),
            device_id_type=MESH)

    def scale(p, b, tangents, send):
        a, w = rspans[p]
        for g in range(2):
            rows = (dot(sel[g], wide(tangents)) * gsl[g]).astype(BF16)
            for h in range(2):
                wsend[b, h, g, :, a:a + w] = rows[:, h * w:(h + 1) * w]
        send()
        for h in range(2):
            for g in range(2):
                wbuf[at.c, b, h, g, mine, a:a + w] = wsend[b, h, g, mine, a:a + w]

    def weigh(_, p):
        a, w = rspans[p]
        tcopy(p).wait_recv()
        tangents = []
        for h in range(2):
            total = tsend[h, :, a:a + w].astype(F32) + trecv[h, :, a:a + w].astype(F32)
            tangents.append(total.astype(BF16))
            if p in wdirect:
                tang[at.b, h, :, a:a + w] = tangents[h]
        if p in wdirect:
            for kind in range(2):
                ucopy(kind, p).start()
        scale(p, at.b, tangents, lambda: out_w.start(*wpiece(p)))
        tan_ref[:, a:a + w] = jnp.where(at.h == 0, tangents[0], tangents[1])

    def others(_, p):
        a, w = rspans[p]
        for kind in range(2):
            ucopy(kind, p).wait_recv()
        scale(p, 1 - at.b, [tang[1 - at.b, h, :, a:a + w] for h in range(2)],
              lambda: out_w2.start(*w2piece(p)))

    def pcopy(kind, p):
        a, w = rspans[p]
        if kind == 0:
            ref = wbuf.at[at.c, at.b, :, :, :, pl.ds(a, w)]
        else:
            ref = wbuf.at[at.c, 1 - at.b, at.chip(3 if kind == 1 else 1) // 2, :, :, pl.ds(a, w)]
        return pltpu.make_async_remote_copy(
            src_ref=ref, dst_ref=ref, send_sem=p_sem.at[0, p, kind],
            recv_sem=p_sem.at[1, p, kind], device_id=at.pair(), device_id_type=MESH)

    def w_one(_, p):
        out_w.wait(*wpiece(p))
        if p not in wdirect:
            out_v.start(*vpiece(p))
        pcopy(0, p).start()

    def w_two(_, p):
        if p in wdirect:
            out_w2.wait(*w2piece(p))
        for kind in range(2):
            if p not in wdirect:
                out_v.copy(kind, *vpiece(p)).wait_recv()
            pcopy(1 + kind, p).start()

    def product(_, p):
        a, w = rspans[p]
        if p == 0:
            for g in range(2):
                hid_t[g] = hid[g, :, own].astype(F32).T.astype(BF16)
        for kind in range(3):
            pcopy(kind, p).wait_recv()
        for k in range(0, 8, 2):
            c, b, h = cbh(k)
            v = sum(dot(hid_t[g], wide([wbuf[c, b, h, g, :, a:a + w] for c in range(2)]))
                    for g in range(2))
            for c in range(2):
                gn_ref[0, :, (k + c) * chunk + a:(k + c) * chunk + a + w] = v[:, c * w:(c + 1) * w]

    for copy in loads[2:]:
        copy.wait()
    pl.semaphore_wait(barrier, experts - 1 + 4)
    steps = {
        "a": choose, "1": d_one, "u": up, "e": exchange, "s": silu, "n": near,
        "h": home, "c": combine, "w": weigh, "v": others, "3": w_one, "4": w_two, "p": product}
    order = plan(dwidths, rwidths, direct, wdirect, *options)[0]
    first_up = [step for step in order if step[0] == "u"][0][1:]
    up_seen = [0, 0]
    for count, (kind, g, p) in enumerate(order):
        steps[kind](g, p)
        if count == 0:
            for k in (0, 1, 2):
                for x in range(4):
                    shared[3 * x + k].start()

    for copy in shared:
        copy.wait_send()
    for g in range(2):
        ecopy(g).wait_send()
        for p in range(nd):
            out_a.drain(*apiece(g, p))
            if (g, p) not in direct:
                out_g.drain(*xpiece(g, p))
    for p in range(nr):
        for g in range(2):
            back.drain(*hpiece(g, p))
            for kind in range(2):
                rcopy(kind, g, p).wait_send()
        tcopy(p).wait_send()
        out_w.drain(*wpiece(p))
        if p in wdirect:
            out_w2.drain(*w2piece(p))
            for kind in range(2):
                ucopy(kind, p).wait_send()
        else:
            out_v.drain(*vpiece(p))
        for kind in range(3):
            pcopy(kind, p).wait_send()


PARTS = 8


def store(gn_ref, tan_ref, gn_out, tan_out, sems):
    rows = gn_ref.shape[1] // PARTS
    copies = [pltpu.make_async_copy(
        gn_ref.at[:, pl.ds(k * rows, rows), :], gn_out.at[:, pl.ds(k * rows, rows), :], sems.at[k])
        for k in range(PARTS)]
    copies.append(pltpu.make_async_copy(tan_ref, tan_out, sems.at[PARTS]))
    for copy in copies:
        copy.start()
    for copy in copies:
        copy.wait()


def on_device(
    dwidths, rwidths, direct, wdirect, cap, options,
    tokens, w_gate, w_up, tangent_down, gates, expert_ids,
):
    experts = lax.axis_size("ep")
    toks, width = tokens.shape
    topk = gates.shape[1]
    chunk = width // 8
    hidden = w_gate.shape[2]
    half = experts * cap
    nd, nr = len(dwidths), len(rwidths)
    vmem, anywhere = pl.BlockSpec(memory_space=pltpu.VMEM), pl.BlockSpec(memory_space=pl.ANY)
    gn, tangent = pl.pallas_call(
        functools.partial(kernel, dwidths, rwidths, direct, wdirect, experts, cap, options),
        out_shape=(
            pltpu.VMEM((1, hidden, width), F32),
            pltpu.VMEM((toks, chunk), BF16),
        ),
        in_specs=[anywhere] * 6,
        out_specs=(vmem, vmem),
        scratch_shapes=[
            pltpu.VMEM((topk, toks), jnp.int32),
            pltpu.VMEM((topk, toks), F32),
            pltpu.VMEM((2, 2, toks, chunk), BF16),
            pltpu.VMEM((4, chunk, 2 * hidden), BF16),
            pltpu.VMEM((4, chunk, 2 * hidden), BF16),
            pltpu.VMEM((4, 2 * hidden, chunk), BF16),
            pltpu.VMEM((2, half, toks), BF16),
            pltpu.VMEM((2, half, toks), F32),
            pltpu.VMEM((2, half, 1), F32),
            pltpu.VMEM((2, toks, half), BF16),
            pltpu.VMEM((2, toks, half), BF16),
            pltpu.VMEM((2, 2, 2, half, chunk), BF16),
            pltpu.VMEM((2, 2, 2, half, chunk), BF16),
            pltpu.VMEM((2, half, 4 * hidden), F32),
            pltpu.VMEM((2, half, 4 * hidden), F32),
            pltpu.VMEM((2, half, 2 * hidden), BF16),
            pltpu.VMEM((2, hidden, half), BF16),
            pltpu.VMEM((2, 2, half, chunk), BF16),
            pltpu.VMEM((2, 2, half, chunk), BF16),
            pltpu.VMEM((2, 2, half, chunk), BF16),
            pltpu.VMEM((2, 2, half, chunk), BF16),
            pltpu.VMEM((2, toks, chunk), BF16),
            pltpu.VMEM((2, toks, chunk), BF16),
            pltpu.VMEM((2, 2, toks, chunk), BF16),
            pltpu.VMEM((2, 2, 2, half, chunk), BF16),
            pltpu.VMEM((2, 2, 2, 2, half, chunk), BF16),
            pltpu.SemaphoreType.DMA((18,)),
            pltpu.SemaphoreType.DMA((2, 12)),
            pltpu.SemaphoreType.DMA((2, 2 * nd)),
            pltpu.SemaphoreType.DMA((2, 2 * nr)),
            pltpu.SemaphoreType.DMA((2, nr)),
            pltpu.SemaphoreType.DMA((2 * nd, 2)),
            pltpu.SemaphoreType.DMA((2 * nd, 2)),
            pltpu.SemaphoreType.DMA((nr, 2)),
            pltpu.SemaphoreType.DMA((nr, 2)),
            pltpu.SemaphoreType.DMA((2, nr, 3)),
            pltpu.SemaphoreType.DMA((2, 2)),
            pltpu.SemaphoreType.DMA((2 * nr, 2)),
            pltpu.SemaphoreType.DMA((2 * nr, 2)),
            pltpu.SemaphoreType.DMA((2, nr)),
            pltpu.SemaphoreType.DMA((2, nr, 2)),
            pltpu.SemaphoreType.DMA((2, nr)),
        ],
        compiler_params=pltpu.CompilerParams(
            collective_id=0, has_side_effects=True, vmem_limit_bytes=50 * 2**20),
    )(expert_ids.T, gates.T, tokens, w_gate, w_up, tangent_down)
    shapes = (
        jax.ShapeDtypeStruct((1, hidden, width), F32), jax.ShapeDtypeStruct((toks, chunk), BF16))
    return pl.pallas_call(
        store,
        out_shape=shapes,
        in_specs=[vmem, vmem],
        out_specs=(anywhere, anywhere),
        scratch_shapes=[pltpu.SemaphoreType.DMA((PARTS + 1,))],
        compiler_params=pltpu.CompilerParams(vmem_limit_bytes=2**20),
    )(*[pltpu.with_memory_space_constraint(v, pltpu.VMEM) for v in (gn, tangent)])


def solution(
    mesh, dwidths=(128,) * 7, rwidths=(128,) * 7, direct=((1, 6),), wdirect=(6,), cap=16,
    options=(),
):
    in_specs = (
        P("ep", None),
        P("ep", None, "fsdp"),
        P("ep", None, "fsdp"),
        P("ep", "fsdp", None),
        P("ep", None),
        P("ep", None),
    )
    out_specs = (P("ep", "fsdp", None), P("ep", "fsdp"))
    return jax.shard_map(
        functools.partial(on_device, dwidths, rwidths, direct, wdirect, cap, options),
        mesh=mesh, in_specs=in_specs, out_specs=out_specs, check_vma=False,
    )
```

```python
import functools

import jax
import jax.numpy as jnp
from jax import lax
from jax.experimental import pallas as pl
from jax.experimental.pallas import tpu as pltpu
from jax.sharding import PartitionSpec as P

MESH = pl.DeviceIdType.MESH
F32 = jnp.float32
BF16 = jnp.bfloat16


def spans(widths):
    out, at = [], 0
    for w in widths:
        out.append((at, w))
        at += w
    return out


def dot(a, b):
    return jnp.dot(a, b, preferred_element_type=F32)


def wide(blocks):
    return jnp.concatenate(blocks, axis=1)


def cbh(k):
    return k % 2, k // 2 % 2, k // 4


class Place:
    def __init__(self):
        self.e = lax.axis_index("ep")
        self.f = lax.axis_index("fsdp")
        self.x = self.f // 2
        self.c = self.f - 2 * self.x
        self.h = self.x // 2
        self.b = self.x - 2 * self.h

    def chip(self, off):
        return lax.rem(self.x + off, 4)

    def chunk(self, off, other=False):
        return 2 * self.chip(off) + (1 - self.c if other else self.c)

    def to(self, off):
        return (self.e, self.chunk(off))

    def pair(self):
        return (self.e, self.chunk(0, True))


class AllToAll:
    def __init__(self, at, experts, cap, src, dst, sems):
        self.__dict__.update(locals())

    def start(self, i, lead, a, w):
        at, cap = self.at, self.cap

        def one(d, carry):
            to = lax.rem(at.e + d, self.experts)
            there = pl.ds(pl.multiple_of(to * cap, cap), cap)
            here = pl.ds(pl.multiple_of(at.e * cap, cap), cap)
            pltpu.make_async_remote_copy(
                src_ref=self.src.at[(*lead, there, pl.ds(a, w))],
                dst_ref=self.dst.at[(*lead, here, pl.ds(a, w))],
                send_sem=self.sems.at[0, i],
                recv_sem=self.sems.at[1, i],
                device_id=(to, at.f),
                device_id_type=MESH,
            ).start()
            return carry

        lax.fori_loop(1, self.experts, one, 0)

    def _all(self, way, i, lead, a, w):
        ref = self.src.at[(*lead, pl.ds(0, (self.experts - 1) * self.cap), pl.ds(a, w))]
        pltpu.make_async_copy(ref, ref, self.sems.at[way, i]).wait()

    def wait(self, *piece):
        self._all(1, *piece)

    def drain(self, *piece):
        self._all(0, *piece)


class Gather:
    def __init__(self, at, buf, send, recv):
        self.__dict__.update(locals())

    def copy(self, kind, i, groups, a, w):
        at = self.at
        ref = self.buf.at[at.b, at.h, groups, :, pl.ds(a, w)]
        return pltpu.make_async_remote_copy(
            src_ref=ref,
            dst_ref=ref,
            send_sem=self.send.at[i, kind],
            recv_sem=self.recv.at[i, kind],
            device_id=at.to(1 if kind == 0 else 3),
            device_id_type=MESH,
        )

    def start(self, *piece):
        for kind in range(2):
            self.copy(kind, *piece).start()

    def wait(self, *piece):
        for kind in range(2):
            self.copy(kind, *piece).wait_recv()

    def drain(self, *piece):
        for kind in range(2):
            self.copy(kind, *piece).wait_send()


def plan(dwidths, rwidths, direct, wdirect, delay=(3.0, 4.0, 2.5)):
    nd, nr = len(dwidths), len(rwidths)
    wd, wr = [w / 896 for w in dwidths], [w / 896 for w in rwidths]
    delay = dict(zip(("x", "yz", "pair"), delay))
    steps = {}
    for g in range(2):
        for p in range(nd):
            w, i = wd[p], g * nd + p
            if (g, p) in direct:
                steps["a", g, p] = (i, 0.4 + 2.4 * w, [], [("yz", 20 * w)])
                steps["u", g, p] = (90 + i, 2.4 * w, [("a", g, p), "weights"], [])
            else:
                steps["a", g, p] = (i, 0.4 + 1.2 * w, [], [("yz", 10 * w)])
                steps["1", g, p] = (i, 0.1, [("a", g, p)], [("x", 10 * w)])
                steps["u", g, p] = (90 + i, 2.4 * w, [("1", g, p), "weights"], [])
        steps["e", g, 0] = (99, 0.1, [("u", g, p) for p in range(nd)], [("pair", 2.0)])
        steps["s", g, 0] = (100, 0.6, [("e", g, 0)], [])
        for p in range(nr):
            w, i = wr[p], 20 + g * nr + p
            steps["n", g, p] = (i, 1.2 * w, [("s", g, 0)], [("x", 10 * w)])
            steps["h", g, p] = (i, 0.4 + 1.4 * w, [("n", g, p)], [("yz", 10 * w)])
    for p in range(nr):
        w, i = wr[p], 40 + p
        steps["c", 0, p] = (i, 1.4 * w, [("h", 0, p), ("h", 1, p)], [("x", 10 * w)])
        if p in wdirect:
            steps["w", 0, p] = (i, 0.4 + 1.6 * w, [("c", 0, p)], [("x", 5 * w), ("yz", 20 * w)])
            steps["v", 0, p] = (i, 0.4 + 1.6 * w, [("x", 0, p)], [("yz", 20 * w)])
            steps["3", 0, p] = (i, 0.1, [("w", 0, p)], [("pair", 4 * w)])
            steps["4", 0, p] = (i, 0.1, [("3", 0, p), ("v", 0, p)], [("pair", 4 * w)])
        else:
            steps["w", 0, p] = (i, 0.4 + 1.6 * w, [("c", 0, p)], [("yz", 20 * w)])
            steps["3", 0, p] = (i, 0.1, [("w", 0, p)], [("x", 20 * w), ("pair", 4 * w)])
            steps["4", 0, p] = (i, 0.1, [("3", 0, p)], [("pair", 4 * w)])
        steps["p", 0, p] = (200 + i, 2.4 * w, [("4", 0, p)], [])
    now, free, order = 0.0, {"x": 0.0, "yz": 0.0, "pair": 0.0}, []
    there = {"weights": 11.0}
    while len(order) < len(steps):
        left = [s for s in steps if s not in there and all(q in there for q in steps[s][2])]
        at = {s: max([there[q] for q in steps[s][2]], default=0.0) for s in left}
        ready = [s for s in left if at[s] <= now]
        if not ready:
            now = min(at.values())
            continue
        step = min(ready, key=lambda s: (steps[s][0], s))
        now += steps[step][1]
        there[step] = now
        for link, time in steps[step][3]:
            free[link] = max(free[link], now) + time
            there[step] = max(there[step], free[link] + delay[link])
            if step[0] == "w" and link == "x":
                there["x", 0, step[2]] = there[step]
        order.append(step)
    return order, now


def kernel(
    dwidths, rwidths, direct, wdirect, experts, cap, options,
    ids_hbm, gates_hbm, tok_ref, wg_ref, wu_ref, td_ref,
    gn_ref, tan_ref,
    ids_ref, gates_ref, tokv, wgv, wuv, tdv, sel, selg, gsl, comb_hi, comb_lo, send, xbuf, acc,
    acc_in, hid, hid_t, rsend, rrecv, fin, ret, tsend, trecv, tang, wsend, wbuf,
    load, v_sem, x_sem, h_sem, w_sem, xg_send, xg_recv, g_send, g_recv, p_sem, e_sem, r_send,
    r_recv, t_sem, u_sem, w2_sem,
):
    at = Place()
    dspans, rspans = spans(dwidths), spans(rwidths)
    nd, nr = len(dspans), len(rspans)
    toks, chunk = tokv.shape[2:]
    hidden = gn_ref.shape[1]
    half = experts * cap
    ranks = 2 * cap
    both = slice(None)
    chips = [(b, h) for h in range(2) for b in range(2)]

    barrier = pltpu.get_barrier_semaphore()

    def greet(d, carry):
        pl.semaphore_signal(
            barrier, inc=1, device_id=(lax.rem(at.e + d, experts), at.f), device_id_type=MESH)
        return carry

    lax.fori_loop(1, experts, greet, 0)
    for to in (at.to(1), at.to(3), at.to(2), at.pair()):
        pl.semaphore_signal(barrier, inc=1, device_id=to, device_id_type=MESH)

    def columns(x, c):
        return pl.ds(pl.multiple_of((2 * x + c) * chunk, 128), chunk)

    own = pl.ds(pl.multiple_of(at.c * hidden, 128), hidden)

    def weights(x, c):
        return [(wg_ref.at[0, columns(x, c), :], wgv.at[x, :, own]),
                (wu_ref.at[0, columns(x, c), :], wuv.at[x, :, own]),
                (td_ref.at[0, :, columns(x, c)], tdv.at[x, own, :])]

    loads = [pltpu.make_async_copy(ids_hbm, ids_ref, load.at[0]),
             pltpu.make_async_copy(gates_hbm, gates_ref, load.at[1])]
    loads += [pltpu.make_async_copy(
        tok_ref.at[:, columns(2 * h + b, at.c)], tokv.at[b, h], load.at[2 + 2 * h + b])
        for b, h in chips]
    local, shared = [], []
    for x in range(4):
        for k, (src, dst) in enumerate(weights(x, at.c)):
            local.append(pltpu.make_async_copy(src, dst, load.at[6 + 3 * x + k]))
        for k, (src, dst) in enumerate(weights(x, 1 - at.c)):
            shared.append(pltpu.make_async_remote_copy(
                src_ref=src, dst_ref=dst, send_sem=v_sem.at[0, 3 * x + k],
                recv_sem=v_sem.at[1, 3 * x + k], device_id=at.pair(), device_id_type=MESH))
    for copy in loads + local:
        copy.start()
    loads[0].wait()
    loads[1].wait()

    expert = lax.broadcasted_iota(jnp.int32, (experts, toks), 0)
    named = [ids_ref[k:k + 1, :] == expert for k in range(ids_ref.shape[0])]
    mask_t = sum(jnp.where(m, 1.0, 0.0) for m in named)
    gate_t = sum(jnp.where(m, gates_ref[k:k + 1, :], 0.0) for k, m in enumerate(named))
    earlier = jnp.where(
        lax.broadcasted_iota(jnp.int32, (toks, toks), 0)
        < lax.broadcasted_iota(jnp.int32, (toks, toks), 1), 1.0, 0.0)
    rank_t = dot(mask_t.astype(BF16), earlier.astype(BF16))
    place = lax.broadcasted_iota(jnp.int32, (ranks, toks), 0).astype(F32)
    for k in range(experts):
        here = (rank_t[k:k + 1, :] == place) & (mask_t[k:k + 1, :] > 0.5)
        picked = jnp.where(here, gate_t[k:k + 1, :], 0.0)
        one = jnp.where(here, 1.0, 0.0).astype(BF16)
        total = jnp.sum(picked, axis=1, keepdims=True)
        for g in range(2):
            r, part = slice(k * cap, (k + 1) * cap), slice(g * cap, (g + 1) * cap)
            sel[g, r, :] = one[part]
            selg[g, r, :] = picked[part]
            gsl[g, r, :] = total[part]

    mine = pl.ds(pl.multiple_of(at.e * cap, cap), cap)
    out_a = AllToAll(at, experts, cap, send, xbuf, x_sem)
    out_g = Gather(at, xbuf, xg_send, xg_recv)
    back = AllToAll(at, experts, cap, fin, ret, h_sem)
    out_w = AllToAll(at, experts, cap, wsend, wbuf.at[at.c], w_sem)
    out_w2 = AllToAll(at, experts, cap, wsend, wbuf.at[at.c], w2_sem)
    out_v = Gather(at, wbuf.at[at.c], g_send, g_recv)

    def apiece(g, p):
        lead = (both, both, g) if (g, p) in direct else (at.b, both, g)
        return g * nd + p, lead, *dspans[p]

    def xpiece(g, p):
        return g * nd + p, g, *dspans[p]

    def hpiece(g, p):
        return g * nr + p, (both, g), *rspans[p]

    def wpiece(p):
        return p, (at.b, both, both), *rspans[p]

    def w2piece(p):
        return p, (1 - at.b, both, both), *rspans[p]

    def vpiece(p):
        return p, both, *rspans[p]

    def choose(g, p):
        if (g, p) != order[0][1:]:
            prepare(g, p)
        out_a.start(*apiece(g, p))
        keep(g, p)

    def which(g, p):
        return chips if (g, p) in direct else [(at.b, h) for h in range(2)]

    def prepare(g, p):
        a, w = dspans[p]
        rows = dot(sel[g], wide([tokv[b, h, :, a:a + w] for b, h in which(g, p)])).astype(BF16)
        for k, (b, h) in enumerate(which(g, p)):
            send[b, h, g, :, a:a + w] = rows[:, k * w:(k + 1) * w]

    def keep(g, p):
        a, w = dspans[p]
        for b, h in which(g, p):
            xbuf[b, h, g, mine, a:a + w] = send[b, h, g, mine, a:a + w]

    def d_one(g, p):
        out_a.wait(*apiece(g, p))
        out_g.start(*xpiece(g, p))

    def up(g, p):
        a, w = dspans[p]
        if (g, p) == first_up:
            for x in range(4):
                for k in range(2):
                    local[3 * x + k].wait()
                    shared[3 * x + k].wait_recv()
        if (g, p) in direct:
            out_a.wait(*apiece(g, p))
        else:
            out_g.wait(*xpiece(g, p))
        for n, matrix in enumerate((wgv, wuv)):
            cols = slice(n * 2 * hidden, (n + 1) * 2 * hidden)
            total = None if up_seen[g] == 0 else acc[g, :, cols]
            for h in range(2):
                part = dot(
                    wide([xbuf[b, h, g, :, a:a + w] for b in range(2)]),
                    jnp.concatenate([matrix[2 * h + b, a:a + w, :] for b in range(2)], axis=0))
                total = part if total is None else total + part
            acc[g, :, cols] = total
        up_seen[g] += 1

    def ecopy(g, m):
        ref, there = (v.at[g, pl.ds(m * half // 2, half // 2), :] for v in (acc, acc_in))
        return pltpu.make_async_remote_copy(
            src_ref=ref, dst_ref=there, send_sem=e_sem.at[0, g, m],
            recv_sem=e_sem.at[1, g, m], device_id=at.pair(), device_id_type=MESH)

    def exchange(g, _):
        for m in range(2):
            ecopy(g, m).start()
        comb = selg[g].T
        hi = comb.astype(BF16)
        comb_hi[g] = hi
        comb_lo[g] = (comb - hi.astype(F32)).astype(BF16)

    def silu(g, _):
        size = 2 * cap if half % (4 * cap) == 0 else cap
        steps = half // 2 // size

        def tile(m, carry):
            r = pl.ds(pl.multiple_of(m * size, size), size)
            v = acc[g, r, :] + acc_in[g, r, :]
            gate, value = v[:, :2 * hidden], v[:, 2 * hidden:]
            hid[g, r, :] = (gate / (1.0 + jnp.exp(-gate)) * value).astype(BF16)
            return carry

        for m in range(2):
            ecopy(g, m).wait_recv()
            lax.fori_loop(m * steps, (m + 1) * steps, tile, 0)
        if g == 0:
            for x in range(4):
                local[3 * x + 2].wait()
                shared[3 * x + 2].wait_recv()

    offs = (1, 3, 2, 0)

    def rcopy(kind, g, p):
        a, w = rspans[p]
        return pltpu.make_async_remote_copy(
            src_ref=rsend.at[kind, g, :, pl.ds(a, w)], dst_ref=rrecv.at[kind, g, :, pl.ds(a, w)],
            send_sem=r_send.at[g * nr + p, kind], recv_sem=r_recv.at[g * nr + p, kind],
            device_id=at.to(1 if kind == 0 else 3), device_id_type=MESH)

    def partial(g, p, js):
        a, w = rspans[p]
        v = dot(hid[g], wide([tdv[at.chip(offs[j]), :, a:a + w] for j in js]))
        return [v[:, i * w:(i + 1) * w] for i in range(len(js))]

    def near(g, p):
        a, w = rspans[p]
        for j, v in enumerate(partial(g, p, (0, 1))):
            rsend[j, g, :, a:a + w] = v.astype(BF16)
            rcopy(j, g, p).start()

    def home(g, p):
        a, w = rspans[p]
        far, v = partial(g, p, (2, 3))
        fin[1 - at.h, g, :, a:a + w] = far.astype(BF16)
        for k in range(2):
            rcopy(k, g, p).wait_recv()
            v += rrecv[k, g, :, a:a + w].astype(F32)
        fin[at.h, g, :, a:a + w] = v.astype(BF16)
        back.start(*hpiece(g, p))
        for h in range(2):
            ret[h, g, mine, a:a + w] = fin[h, g, mine, a:a + w]

    def tcopy(p):
        a, w = rspans[p]
        return pltpu.make_async_remote_copy(
            src_ref=tsend.at[:, :, pl.ds(a, w)], dst_ref=trecv.at[:, :, pl.ds(a, w)],
            send_sem=t_sem.at[0, p], recv_sem=t_sem.at[1, p],
            device_id=at.to(2), device_id_type=MESH)

    def combine(_, p):
        a, w = rspans[p]
        for g in range(2):
            back.wait(*hpiece(g, p))
        total = jnp.zeros((toks, 2 * w), F32)
        for g in range(2):
            got = wide([ret[h, g, :, a:a + w] for h in range(2)])
            total += dot(comb_hi[g], got) + dot(comb_lo[g], got)
        for h in range(2):
            tsend[h, :, a:a + w] = total[:, h * w:(h + 1) * w].astype(BF16)
        tcopy(p).start()

    def ucopy(kind, p):
        a, w = rspans[p]
        ref = tang.at[at.b, at.h, :, pl.ds(a, w)]
        return pltpu.make_async_remote_copy(
            src_ref=ref, dst_ref=ref, send_sem=u_sem.at[0, p, kind],
            recv_sem=u_sem.at[1, p, kind], device_id=at.to(1 if kind == 0 else 3),
            device_id_type=MESH)

    def scale(p, b, tangents, send):
        a, w = rspans[p]
        for g in range(2):
            rows = (dot(sel[g], wide(tangents)) * gsl[g]).astype(BF16)
            for h in range(2):
                wsend[b, h, g, :, a:a + w] = rows[:, h * w:(h + 1) * w]
        send()
        for h in range(2):
            for g in range(2):
                wbuf[at.c, b, h, g, mine, a:a + w] = wsend[b, h, g, mine, a:a + w]

    def weigh(_, p):
        a, w = rspans[p]
        tcopy(p).wait_recv()
        tangents = []
        for h in range(2):
            total = tsend[h, :, a:a + w].astype(F32) + trecv[h, :, a:a + w].astype(F32)
            tangents.append(total.astype(BF16))
            if p in wdirect:
                tang[at.b, h, :, a:a + w] = tangents[h]
        if p in wdirect:
            for kind in range(2):
                ucopy(kind, p).start()
        scale(p, at.b, tangents, lambda: out_w.start(*wpiece(p)))
        tan_ref[:, a:a + w] = jnp.where(at.h == 0, tangents[0], tangents[1])

    def others(_, p):
        a, w = rspans[p]
        for kind in range(2):
            ucopy(kind, p).wait_recv()
        scale(p, 1 - at.b, [tang[1 - at.b, h, :, a:a + w] for h in range(2)],
              lambda: out_w2.start(*w2piece(p)))

    def pcopy(kind, p):
        a, w = rspans[p]
        if kind == 0:
            ref = wbuf.at[at.c, at.b, :, :, :, pl.ds(a, w)]
        else:
            ref = wbuf.at[at.c, 1 - at.b, at.chip(3 if kind == 1 else 1) // 2, :, :, pl.ds(a, w)]
        return pltpu.make_async_remote_copy(
            src_ref=ref, dst_ref=ref, send_sem=p_sem.at[0, p, kind],
            recv_sem=p_sem.at[1, p, kind], device_id=at.pair(), device_id_type=MESH)

    def w_one(_, p):
        out_w.wait(*wpiece(p))
        if p not in wdirect:
            out_v.start(*vpiece(p))
        pcopy(0, p).start()

    def w_two(_, p):
        if p in wdirect:
            out_w2.wait(*w2piece(p))
        for kind in range(2):
            if p not in wdirect:
                out_v.copy(kind, *vpiece(p)).wait_recv()
            pcopy(1 + kind, p).start()

    def product(_, p):
        a, w = rspans[p]
        if p == 0:
            for g in range(2):
                hid_t[g] = hid[g, :, own].astype(F32).T.astype(BF16)
        for kind in range(3):
            pcopy(kind, p).wait_recv()
        for k in range(0, 8, 2):
            c, b, h = cbh(k)
            v = sum(dot(hid_t[g], wide([wbuf[c, b, h, g, :, a:a + w] for c in range(2)]))
                    for g in range(2))
            for c in range(2):
                gn_ref[0, :, (k + c) * chunk + a:(k + c) * chunk + a + w] = v[:, c * w:(c + 1) * w]

    order = plan(dwidths, rwidths, direct, wdirect, *options)[0]
    for copy in loads[2:]:
        copy.wait()
    prepare(*order[0][1:])
    pl.semaphore_wait(barrier, experts - 1 + 4)
    steps = {
        "a": choose, "1": d_one, "u": up, "e": exchange, "s": silu, "n": near,
        "h": home, "c": combine, "w": weigh, "v": others, "3": w_one, "4": w_two, "p": product}
    first_up = [step for step in order if step[0] == "u"][0][1:]
    up_seen = [0, 0]
    for count, (kind, g, p) in enumerate(order):
        steps[kind](g, p)
        if count == 0:
            for k in (0, 1, 2):
                for x in range(4):
                    shared[3 * x + k].start()

    for copy in shared:
        copy.wait_send()
    for g in range(2):
        for m in range(2):
            ecopy(g, m).wait_send()
        for p in range(nd):
            out_a.drain(*apiece(g, p))
            if (g, p) not in direct:
                out_g.drain(*xpiece(g, p))
    for p in range(nr):
        for g in range(2):
            back.drain(*hpiece(g, p))
            for kind in range(2):
                rcopy(kind, g, p).wait_send()
        tcopy(p).wait_send()
        out_w.drain(*wpiece(p))
        if p in wdirect:
            out_w2.drain(*w2piece(p))
            for kind in range(2):
                ucopy(kind, p).wait_send()
        else:
            out_v.drain(*vpiece(p))
        for kind in range(3):
            pcopy(kind, p).wait_send()


PARTS = 8


def store(gn_ref, tan_ref, gn_out, tan_out, sems):
    rows = gn_ref.shape[1] // PARTS
    copies = [pltpu.make_async_copy(
        gn_ref.at[:, pl.ds(k * rows, rows), :], gn_out.at[:, pl.ds(k * rows, rows), :], sems.at[k])
        for k in range(PARTS)]
    copies.append(pltpu.make_async_copy(tan_ref, tan_out, sems.at[PARTS]))
    for copy in copies:
        copy.start()
    for copy in copies:
        copy.wait()


def on_device(
    dwidths, rwidths, direct, wdirect, cap, options,
    tokens, w_gate, w_up, tangent_down, gates, expert_ids,
):
    experts = lax.axis_size("ep")
    toks, width = tokens.shape
    topk = gates.shape[1]
    chunk = width // 8
    hidden = w_gate.shape[2]
    half = experts * cap
    nd, nr = len(dwidths), len(rwidths)
    vmem, anywhere = pl.BlockSpec(memory_space=pltpu.VMEM), pl.BlockSpec(memory_space=pl.ANY)
    gn, tangent = pl.pallas_call(
        functools.partial(kernel, dwidths, rwidths, direct, wdirect, experts, cap, options),
        out_shape=(
            pltpu.VMEM((1, hidden, width), F32),
            pltpu.VMEM((toks, chunk), BF16),
        ),
        in_specs=[anywhere] * 6,
        out_specs=(vmem, vmem),
        scratch_shapes=[
            pltpu.VMEM((topk, toks), jnp.int32),
            pltpu.VMEM((topk, toks), F32),
            pltpu.VMEM((2, 2, toks, chunk), BF16),
            pltpu.VMEM((4, chunk, 2 * hidden), BF16),
            pltpu.VMEM((4, chunk, 2 * hidden), BF16),
            pltpu.VMEM((4, 2 * hidden, chunk), BF16),
            pltpu.VMEM((2, half, toks), BF16),
            pltpu.VMEM((2, half, toks), F32),
            pltpu.VMEM((2, half, 1), F32),
            pltpu.VMEM((2, toks, half), BF16),
            pltpu.VMEM((2, toks, half), BF16),
            pltpu.VMEM((2, 2, 2, half, chunk), BF16),
            pltpu.VMEM((2, 2, 2, half, chunk), BF16),
            pltpu.VMEM((2, half, 4 * hidden), F32),
            pltpu.VMEM((2, half, 4 * hidden), F32),
            pltpu.VMEM((2, half, 2 * hidden), BF16),
            pltpu.VMEM((2, hidden, half), BF16),
            pltpu.VMEM((2, 2, half, chunk), BF16),
            pltpu.VMEM((2, 2, half, chunk), BF16),
            pltpu.VMEM((2, 2, half, chunk), BF16),
            pltpu.VMEM((2, 2, half, chunk), BF16),
            pltpu.VMEM((2, toks, chunk), BF16),
            pltpu.VMEM((2, toks, chunk), BF16),
            pltpu.VMEM((2, 2, toks, chunk), BF16),
            pltpu.VMEM((2, 2, 2, half, chunk), BF16),
            pltpu.VMEM((2, 2, 2, 2, half, chunk), BF16),
            pltpu.SemaphoreType.DMA((18,)),
            pltpu.SemaphoreType.DMA((2, 12)),
            pltpu.SemaphoreType.DMA((2, 2 * nd)),
            pltpu.SemaphoreType.DMA((2, 2 * nr)),
            pltpu.SemaphoreType.DMA((2, nr)),
            pltpu.SemaphoreType.DMA((2 * nd, 2)),
            pltpu.SemaphoreType.DMA((2 * nd, 2)),
            pltpu.SemaphoreType.DMA((nr, 2)),
            pltpu.SemaphoreType.DMA((nr, 2)),
            pltpu.SemaphoreType.DMA((2, nr, 3)),
            pltpu.SemaphoreType.DMA((2, 2, 2)),
            pltpu.SemaphoreType.DMA((2 * nr, 2)),
            pltpu.SemaphoreType.DMA((2 * nr, 2)),
            pltpu.SemaphoreType.DMA((2, nr)),
            pltpu.SemaphoreType.DMA((2, nr, 2)),
            pltpu.SemaphoreType.DMA((2, nr)),
        ],
        compiler_params=pltpu.CompilerParams(
            collective_id=0, has_side_effects=True, vmem_limit_bytes=50 * 2**20),
    )(expert_ids.T, gates.T, tokens, w_gate, w_up, tangent_down)
    shapes = (
        jax.ShapeDtypeStruct((1, hidden, width), F32), jax.ShapeDtypeStruct((toks, chunk), BF16))
    return pl.pallas_call(
        store,
        out_shape=shapes,
        in_specs=[vmem, vmem],
        out_specs=(anywhere, anywhere),
        scratch_shapes=[pltpu.SemaphoreType.DMA((PARTS + 1,))],
        compiler_params=pltpu.CompilerParams(vmem_limit_bytes=2**20),
    )(*[pltpu.with_memory_space_constraint(v, pltpu.VMEM) for v in (gn, tangent)])


def solution(
    mesh, dwidths=(128,) * 7, rwidths=(128,) * 7, direct=((1, 4), (1, 5), (1, 6)), wdirect=(6,), cap=16,
    options=(),
):
    in_specs = (
        P("ep", None),
        P("ep", None, "fsdp"),
        P("ep", None, "fsdp"),
        P("ep", "fsdp", None),
        P("ep", None),
        P("ep", None),
    )
    out_specs = (P("ep", "fsdp", None), P("ep", "fsdp"))
    return jax.shard_map(
        functools.partial(on_device, dwidths, rwidths, direct, wdirect, cap, options),
        mesh=mesh, in_specs=in_specs, out_specs=out_specs, check_vma=False,
    )
```
